256 devices in a mesh: visit: 32 (over y, z), tile: 8 (over x, core).
Axes of the slice: x: 4, y: 4, z: 8, core: 2. Of those that a mesh axis runs over, the one named last changes fastest.
Arguments:
- visit_image: bfloat16 [32, 2048, 2048], P('visit', 'tile'), may hold values from -6 to 6
- good_mask: int32 [32, 2048, 2048], P('visit', 'tile'), may hold values 0 or 1
- basis_rows: float32 [27, 21], replicated, may hold values from -1.25 to 1.25
- basis_cols: float32 [27, 21], replicated, may hold values from -1.25 to 1.25
- visit_coeff: float32 [32, 27], P('visit'), may hold values from -1.25 to 1.25
- visit_weight: float32 [32], P('visit'), may hold values from 0.25 to 4
- col_offset: int32 [32], P('visit'), may hold values from -64 to 64
- patch_of: int32 [32, 1], replicated, may hold values from 0 to 7
- new_image: bfloat16 [32, 2048, 2048], P('visit', 'tile'), may hold values from -6 to 6
- new_coeff: float32 [32, 27], P('visit'), may hold values from -1.25 to 1.25
- new_patch: int32 [32, 1], replicated, may hold values from 0 to 7
Outputs:
- coadd: bfloat16 [8, 8, 256, 2048], P(None, 'tile', 'visit')
- difference: float32 [32, 2048, 2048], P('visit', 'tile')
The draws below stay inside these ranges and needn't reach their ends.
Inputs may be any that keep to these rules, and one draw needn't show every extreme that they name: `patch_of`: every one of the 8 patches is intersected by at least one visit. `new_patch`: every one of the 8 patches lies under at least one new visit.
All inputs are finite; a program needn't handle non-finite values. No bound on the sum of `good_mask` on one device may be relied on, other than what follows from the above.
Results may differ from the reference program's by a relative error of at most 0.007.
Values may be sent and summed in bfloat16 or wider, within the bound.
No kernel may reach another device: no remote copies, remote signals or barrier semaphores. Data moves between devices by JAX's collectives and lax.ppermute only.
A program may use at most 128 MiB of HBM per device.

```python
import math
import jax
import jax.numpy as jnp
from jax import lax

KS = 21
NB = 27
W = 2048
ROWS_DEV = 256
PATCHES = 8
OFF = 64
VISITS = 32
NEWV = 32
TILES = 8
H = 2048


def plant(drawn, rng, low, high):
    longest = drawn.shape.index(max(drawn.shape))
    spots = []
    for shift in (0, 1):
        where = [jax.random.randint(jax.random.fold_in(rng, axis), (), 0, length) for axis, length in enumerate(drawn.shape)]
        where[longest] = (where[longest] + shift) % drawn.shape[longest]
        spots.append(tuple(where))
    return drawn.at[spots[0]].set(low).at[spots[1]].set(high)


def block_levels(rng, extent, pieces, smallest, largest):
    loudness = 1.0
    for dim, parts in pieces:
        heights = jax.random.uniform(jax.random.fold_in(jax.random.fold_in(rng, 6), dim), (parts,), jnp.float32, smallest / len(pieces), largest / len(pieces))
        loudness = loudness * jnp.repeat(jnp.exp(heights), extent[dim] // parts).reshape((-1,) + (1,) * (len(extent) - 1 - dim))
    return loudness


def picks_of(own_key, rows, number_of, top, lift):
    sequence = jax.random.permutation(jax.random.fold_in(own_key, 1), number_of)
    boost = sequence
    for power in range(3):
        boost = boost * boost // number_of
    boost = boost * lift // number_of
    lots = jax.random.randint(jax.random.fold_in(own_key, 2), (rows, number_of), 0, 4096) + boost
    holders = jax.random.permutation(jax.random.fold_in(own_key, 3), rows)[jnp.arange(number_of) % rows]
    lots = jnp.where(jnp.arange(rows)[:, None] == holders[None, :], 1 << 14, lots)
    score = lots * number_of + jnp.arange(number_of)
    return lax.top_k(score.astype(jnp.int32), top)[1].astype(jnp.int32)


def noise(own_key, shape, deviation, bound, pieces=(), held_as=jnp.bfloat16):
    gain = block_levels(own_key, shape, pieces, -0.22, 0.18) if pieces else 1.0
    values = jax.random.normal(own_key, shape, jnp.float32) * deviation * gain
    return jnp.minimum(jnp.maximum(values, -bound), bound).astype(held_as)


def setup_inputs(seed: int = 0) -> dict:
    key_of = jax.random.split(jax.random.key(seed), 12)
    return {
        "visit_image": noise(key_of[0], (VISITS, H, W), 1.0, 6.0, ((0, 32), (1, 8))),
        "good_mask": plant((jax.random.randint(key_of[1], (VISITS, H, W), 0, 8) < 7).astype(jnp.int32), jax.random.fold_in(key_of[1], 1), 0, 1),
        "basis_rows": noise(key_of[2], (NB, KS), KS ** -0.5, 1.25, (), jnp.float32),
        "basis_cols": noise(key_of[3], (NB, KS), KS ** -0.5, 1.25, (), jnp.float32),
        "visit_coeff": noise(key_of[4], (VISITS, NB), NB ** -0.5, 1.25, ((0, 32),), jnp.float32),
        "visit_weight": jnp.clip(jnp.exp(math.log(4.0) - 2.7725887 * jax.random.uniform(key_of[5], (VISITS,), jnp.float32) ** block_levels(key_of[5], (VISITS,), ((0, 32),), -0.2, 0.2)), 0.25, 4.0),
        "col_offset": plant(jax.random.randint(key_of[6], (VISITS,), 0 - OFF, OFF + 1), jax.random.fold_in(key_of[6], 1), 0 - OFF, OFF).astype(jnp.int32),
        "patch_of": picks_of(key_of[7], VISITS, PATCHES, 1, 2048),
        "new_image": noise(key_of[8], (NEWV, H, W), 1.0, 6.0, ((0, 32), (1, 8))),
        "new_coeff": noise(key_of[9], (NEWV, NB), NB ** -0.5, 1.25, ((0, 32),), jnp.float32),
        "new_patch": picks_of(key_of[10], NEWV, PATCHES, 1, 1024),
    }


def build_kernel(coefficients, basis_rows, basis_cols):
    summed = jnp.sum(coefficients[:, None, None] * basis_rows[:, :, None] * basis_cols[:, None, :], axis=0)
    return summed.astype(jnp.bfloat16)


def convolve(picture, kernel):
    halfwidth = KS // 2
    source = picture.astype(jnp.float32)[None, None]
    weights = kernel.astype(jnp.float32)[None, None]
    result = lax.conv_general_dilated(source, weights, (1, 1), ((halfwidth, halfwidth), (halfwidth, halfwidth)), precision=lax.Precision.HIGHEST)
    return result[0, 0]


def reference(visit_image, good_mask, basis_rows, basis_cols, visit_coeff, visit_weight, col_offset, patch_of, new_image, new_coeff, new_patch):
    def match_visit(carry, inputs):
        numerator, denominator = carry
        visit_pixels, good_pixels, coefficients, weight, offset, patch_id = inputs
        matched = convolve(visit_pixels, build_kernel(coefficients, basis_rows, basis_cols))
        first_col = (OFF - offset).astype(jnp.int32)
        placed = lax.dynamic_slice_in_dim(jnp.pad(matched, ((0, 0), (OFF, OFF))), first_col, W, 1)
        inside = lax.dynamic_slice_in_dim(jnp.pad(good_pixels.astype(jnp.float32), ((0, 0), (OFF, OFF))), first_col, W, 1)
        coverage = weight * inside
        weighted = lax.optimization_barrier((placed * coverage).astype(jnp.bfloat16))
        cover_rounded = lax.optimization_barrier(coverage.astype(jnp.bfloat16))
        numerator = numerator.at[patch_id].add(weighted.astype(jnp.float32))
        denominator = denominator.at[patch_id].add(cover_rounded.astype(jnp.float32))
        return (numerator, denominator), None

    empty_sum = jnp.zeros((PATCHES, H, W), jnp.float32)
    (numerator, denominator), _ = lax.scan(match_visit, (empty_sum, empty_sum), (visit_image, good_mask, visit_coeff, visit_weight, col_offset, patch_of[:, 0]))
    coadd = (numerator / jnp.maximum(denominator, 1.0)).astype(jnp.bfloat16)

    def subtract(inputs):
        new_pixels, coefficients, patch_id = inputs
        template = lax.dynamic_index_in_dim(coadd, patch_id, 0, keepdims=False)
        return new_pixels.astype(jnp.float32) - convolve(template, build_kernel(coefficients, basis_rows, basis_cols))

    difference = lax.map(subtract, (new_image, new_coeff, new_patch[:, 0]))
    return coadd.reshape(PATCHES, TILES, ROWS_DEV, W), difference
```

```python
import functools

import jax
import jax.numpy as jnp
from jax import lax
from jax.experimental import pallas as pl
from jax.experimental.pallas import tpu as pltpu
from jax.sharding import PartitionSpec as P

KS = 21
HALF = KS // 2
PATCHES = 8
LANES = 128
HALO = 16
QUAD = 4
SPLIT = LANES // 2
SHIFTS = QUAD + KS - 1
STRIDE = 16
PLANES = STRIDE - QUAD + SHIFTS
VMEM_LIMIT = 56 * 2**20


def neighbours(block, axis):
    count = lax.axis_size(axis)
    forward = [(i, i + 1) for i in range(count - 1)]
    backward = [(target, source) for source, target in forward]
    low = lax.ppermute(block[-HALO:], axis, forward)
    high = lax.ppermute(block[:HALO], axis, backward)
    return low, high


def table_kernel(rows_ref, cols_ref, first_ref, second_ref, *table_refs):
    tap = lax.broadcasted_iota(jnp.int32, (KS, QUAD * SPLIT), 0)
    place = lax.broadcasted_iota(jnp.int32, (KS, QUAD * SPLIT), 1)
    shift = lax.broadcasted_iota(jnp.int32, (SHIFTS, KS), 0)
    row_tap = lax.broadcasted_iota(jnp.int32, (SHIFTS, KS), 1)
    lane = lax.broadcasted_iota(jnp.int32, (LANES, QUAD * SPLIT), 0)
    column = lax.broadcasted_iota(jnp.int32, (LANES, QUAD * SPLIT), 1) % SPLIT
    inside = (lane >= column) & (lane - column < KS)
    for coeff_ref, table_ref in zip((first_ref, second_ref), table_refs):
        kernel = lax.dot_general(
            rows_ref[...] * coeff_ref[...],
            cols_ref[...],
            (((0,), (0,)), ((), ())),
            precision=lax.Precision.HIGHEST,
            preferred_element_type=jnp.float32,
        ).astype(jnp.bfloat16)
        profile = jnp.zeros((SHIFTS, QUAD * SPLIT), jnp.float32)
        for e in range(QUAD):
            at = (SPLIT * e - tap) % (QUAD * SPLIT)
            spread = jnp.dot(
                kernel, (place == at).astype(jnp.bfloat16), preferred_element_type=jnp.float32
            )
            lowered = (shift - e == row_tap).astype(jnp.bfloat16)
            profile = profile + jnp.dot(
                lowered, spread.astype(jnp.bfloat16), preferred_element_type=jnp.float32
            )
        for s in range(SHIFTS):
            wide = jnp.broadcast_to(profile[s : s + 1], (LANES, QUAD * SPLIT))
            rolled = pltpu.roll(wide, 0, 1, stride=1, stride_axis=0)
            table_ref[s * LANES : (s + 1) * LANES, :] = jnp.where(inside, rolled, 0.0).astype(
                jnp.bfloat16
            )


def build_tables(basis_rows, basis_cols, visit_coeff, new_coeff):
    table = jax.ShapeDtypeStruct((SHIFTS * LANES, QUAD * SPLIT), jnp.bfloat16)
    return pl.pallas_call(
        table_kernel,
        out_shape=(table, table),
        compiler_params=pltpu.CompilerParams(vmem_limit_bytes=VMEM_LIMIT),
        cost_estimate=pl.CostEstimate(flops=10**9, bytes_accessed=4 * 10**6, transcendentals=0),
        name="tables",
    )(basis_rows, basis_cols, visit_coeff.reshape(-1, 1), new_coeff.reshape(-1, 1))


def shifted_block(load, blocks, h, shift, lane):
    turn = lax.rem(shift + 2 * LANES, LANES)
    back = (turn - shift) // LANES

    def rolled(j):
        clamped = jnp.clip(j, 0, blocks - 1)
        block = pltpu.roll(load(clamped), turn, 1)
        return jnp.where(clamped == j, block, jnp.zeros_like(block))

    return jnp.where(lane >= turn, rolled(h + back), rolled(h + back - 1))


def convolve(low_ref, mid_ref, high_ref, table_ref, shift, moved_ref, planes_ref, matched_ref):
    height, columns = mid_ref.shape
    blocks = columns // LANES
    chunk = 64
    for align in range(2):
        for source, first, count in (
            (low_ref, 0, HALO),
            *((mid_ref.at[pl.ds(r, chunk)], HALO + r, chunk) for r in range(0, height, chunk)),
            (high_ref, HALO + height, HALO),
        ):
            lane = lax.broadcasted_iota(jnp.int32, (count, LANES), 1)

            def load(j, source=source):
                return source[:, pl.ds(pl.multiple_of(j * LANES, LANES), LANES)].astype(jnp.float32)

            for h in range(blocks):
                moved_ref[2 * h + align, first : first + count, :] = shifted_block(
                    load, blocks, h, shift + HALF - align * SPLIT, lane
                )
    per = height // STRIDE
    for g in range(2 * blocks):
        for s in range(PLANES):
            planes_ref[s, g * per : (g + 1) * per, :] = moved_ref[
                g, pl.ds(HALO - HALF + s, per, stride=STRIDE), :
            ].astype(jnp.bfloat16)
    lane = lax.broadcasted_iota(jnp.int32, (per, LANES), 1)
    for i in range(STRIDE // QUAD):
        left = jnp.concatenate([planes_ref[QUAD * i + s] for s in range(SHIFTS)], axis=1)
        product = jnp.dot(left, table_ref[...], preferred_element_type=jnp.float32)
        for h in range(blocks):
            for pair in range(QUAD // 2):
                lanes = slice(pair * LANES, (pair + 1) * LANES)
                a = product[2 * h * per : (2 * h + 1) * per, lanes]
                b = product[(2 * h + 1) * per : (2 * h + 2) * per, lanes]
                row = QUAD * i + 2 * pair
                matched_ref[h, pl.ds(row, per, stride=STRIDE), :] = jnp.where(
                    lane < SPLIT, a, pltpu.roll(b, SPLIT, 1)
                )
                matched_ref[h, pl.ds(row + 1, per, stride=STRIDE), :] = jnp.where(
                    lane < SPLIT, pltpu.roll(a, SPLIT, 1), b
                )


def visit_kernel(
    offset_ref, weight_ref, low_ref, mid_ref, high_ref, mask_ref, table_ref, out_ref, moved, planes, matched
):
    offset = offset_ref[0]
    weight = weight_ref[0]
    convolve(low_ref, mid_ref, high_ref, table_ref, offset, moved, planes, matched)
    height, columns = mid_ref.shape
    blocks = columns // LANES
    owners, double, _ = out_ref.shape
    rows = double // 2
    lane = lax.broadcasted_iota(jnp.int32, (rows, LANES), 1)
    for d in range(owners):

        def load(j, d=d):
            return mask_ref[
                d * rows : (d + 1) * rows, pl.ds(pl.multiple_of(j * LANES, LANES), LANES)
            ]

        for h in range(blocks):
            good = shifted_block(load, blocks, h, offset, lane)
            coverage = weight * good.astype(jnp.float32)
            weighted = coverage * matched[h, d * rows : (d + 1) * rows, :]
            out_ref[d, :, h * LANES : (h + 1) * LANES] = jnp.concatenate(
                [weighted, coverage], axis=0
            ).astype(jnp.bfloat16)


def new_kernel(low_ref, mid_ref, high_ref, new_ref, table_ref, out_ref, moved, planes, matched):
    convolve(low_ref, mid_ref, high_ref, table_ref, jnp.int32(0), moved, planes, matched)
    blocks = out_ref.shape[1] // LANES
    for h in range(blocks):
        lanes = slice(h * LANES, (h + 1) * LANES)
        out_ref[:, lanes] = new_ref[:, lanes].astype(jnp.float32) - matched[h]


def conv_scratch(height, columns):
    blocks = columns // LANES
    return [
        pltpu.VMEM((2 * blocks, height + 2 * HALO, LANES), jnp.float32),
        pltpu.VMEM((PLANES, 2 * blocks * (height // STRIDE), LANES), jnp.bfloat16),
        pltpu.VMEM((blocks, height, LANES), jnp.float32),
    ]


def conv_cost(height, columns):
    return pl.CostEstimate(
        flops=2 * height * columns * SHIFTS * LANES, bytes_accessed=8 * 10**6, transcendentals=0
    )


def match_visit(low, mid, high, mask, table, offset, weight, owners):
    height, columns = mid.shape
    smem = pl.BlockSpec(memory_space=pltpu.SMEM)
    vmem = pl.BlockSpec(memory_space=pltpu.VMEM)
    return pl.pallas_call(
        visit_kernel,
        out_shape=jax.ShapeDtypeStruct((owners, 2 * (height // owners), columns), jnp.bfloat16),
        in_specs=[smem, smem] + [vmem] * 5,
        out_specs=vmem,
        scratch_shapes=conv_scratch(height, columns),
        compiler_params=pltpu.CompilerParams(vmem_limit_bytes=VMEM_LIMIT),
        cost_estimate=conv_cost(height, columns),
        name="match_visit",
    )(offset, weight, low, mid, high, mask, table)


def subtract(low, mid, high, new, table):
    height, columns = mid.shape
    vmem = pl.BlockSpec(memory_space=pltpu.VMEM)
    return pl.pallas_call(
        new_kernel,
        out_shape=jax.ShapeDtypeStruct((height, columns), jnp.float32),
        in_specs=[vmem] * 5,
        out_specs=vmem,
        scratch_shapes=conv_scratch(height, columns),
        compiler_params=pltpu.CompilerParams(vmem_limit_bytes=VMEM_LIMIT),
        cost_estimate=conv_cost(height, columns),
        name="subtract",
    )(low, mid, high, new, table)


def coadd_kernel(patch_ref, wanted_ref, received_ref, coadd_ref, send_ref, sums):
    visits, double, columns = received_ref.shape
    rows = double // 2
    sums[...] = jnp.zeros_like(sums)

    def add(v, carry):
        p = patch_ref[v]
        sums[p] = sums[p] + received_ref[v].astype(jnp.float32)
        return carry

    lax.fori_loop(0, visits, add, 0)
    for p in range(PATCHES):
        coadd_ref[p] = (sums[p, :rows] / jnp.maximum(sums[p, rows:], 1.0)).astype(jnp.bfloat16)

    def place(n, carry):
        send_ref[n] = coadd_ref[wanted_ref[n]]
        return carry

    lax.fori_loop(0, send_ref.shape[0], place, 0)


def combine(received, patch_of, new_patch):
    visits, double, columns = received.shape
    rows = double // 2
    smem = pl.BlockSpec(memory_space=pltpu.SMEM)
    vmem = pl.BlockSpec(memory_space=pltpu.VMEM)
    return pl.pallas_call(
        coadd_kernel,
        out_shape=(
            jax.ShapeDtypeStruct((PATCHES, rows, columns), jnp.bfloat16),
            jax.ShapeDtypeStruct((new_patch.shape[0], rows, columns), jnp.bfloat16),
        ),
        in_specs=[smem, smem, vmem],
        out_specs=(vmem, vmem),
        scratch_shapes=[pltpu.VMEM((PATCHES, double, columns), jnp.float32)],
        compiler_params=pltpu.CompilerParams(vmem_limit_bytes=VMEM_LIMIT),
        name="combine",
    )(patch_of, new_patch, received)


def per_device(
    visit_image,
    good_mask,
    basis_rows,
    basis_cols,
    visit_coeff,
    visit_weight,
    col_offset,
    patch_of,
    new_image,
    new_coeff,
    new_patch,
):
    owners = lax.axis_size("visit")
    low, high = neighbours(visit_image[0], "tile")
    visit_table, new_table = build_tables(basis_rows, basis_cols, visit_coeff, new_coeff)
    outgoing = match_visit(
        low, visit_image[0], high, good_mask[0], visit_table, col_offset, visit_weight, owners
    )
    received = lax.all_to_all(outgoing, "visit", split_axis=0, concat_axis=0, tiled=True)
    coadd, wanted = combine(received, patch_of[:, 0], new_patch[:, 0])
    template = lax.all_to_all(wanted, "visit", split_axis=0, concat_axis=0, tiled=True)
    template = template.reshape(new_image.shape[1:])
    low, high = neighbours(template, "tile")
    difference = subtract(low, template, high, new_image[0], new_table)
    return (coadd[:, None], difference[None])


def solution(mesh):
    return jax.shard_map(
        per_device,
        mesh=mesh,
        in_specs=(
            P("visit", "tile", None),
            P("visit", "tile", None),
            P(),
            P(),
            P("visit", None),
            P("visit"),
            P("visit"),
            P(),
            P("visit", "tile", None),
            P("visit", None),
            P(),
        ),
        out_specs=(P(None, "tile", "visit", None), P("visit", "tile", None)),
        check_vma=False,
    )
```

```python
import jax
import jax.numpy as jnp
from jax import lax
from jax.experimental import pallas as pl
from jax.experimental.pallas import tpu as pltpu
from jax.sharding import PartitionSpec as P

KS = 21
HALF = KS // 2
PATCHES = 8
LANES = 128
HALO = 16
QUAD = 4
SPLIT = LANES // 2
SHIFTS = QUAD + KS - 1
CHUNK = 64
VMEM_LIMIT = 24 * 2**20


def params():
    return pltpu.CompilerParams(vmem_limit_bytes=VMEM_LIMIT)


def neighbours(block, axis):
    count = lax.axis_size(axis)
    forward = [(i, i + 1) for i in range(count - 1)]
    backward = [(target, source) for source, target in forward]
    low = lax.ppermute(block[-HALO:], axis, forward)
    high = lax.ppermute(block[:HALO], axis, backward)
    return low, high


def table_kernel(rows_ref, cols_ref, first_ref, second_ref, *table_refs):
    wide = QUAD * SPLIT
    tap = lax.broadcasted_iota(jnp.int32, (KS, wide), 0)
    place = lax.broadcasted_iota(jnp.int32, (KS, wide), 1)
    shift = lax.broadcasted_iota(jnp.int32, (SHIFTS, KS), 0)
    row_tap = lax.broadcasted_iota(jnp.int32, (SHIFTS, KS), 1)
    lane = lax.broadcasted_iota(jnp.int32, (LANES, wide), 0)
    column = lax.broadcasted_iota(jnp.int32, (LANES, wide), 1) % SPLIT
    inside = (lane >= column) & (lane - column < KS)
    for coeff_ref, table_ref in zip((first_ref, second_ref), table_refs):
        kernel = lax.dot_general(
            rows_ref[...] * coeff_ref[...],
            cols_ref[...],
            (((1,), (1,)), ((), ())),
            precision=lax.Precision.HIGHEST,
            preferred_element_type=jnp.float32,
        ).astype(jnp.bfloat16)
        profile = jnp.zeros((SHIFTS, wide), jnp.float32)
        for e in range(QUAD):
            at = (SPLIT * e - tap) % wide
            spread = jnp.dot(
                kernel, (place == at).astype(jnp.bfloat16), preferred_element_type=jnp.float32
            )
            lowered = (shift - e == row_tap).astype(jnp.bfloat16)
            profile = profile + jnp.dot(
                lowered, spread.astype(jnp.bfloat16), preferred_element_type=jnp.float32
            )
        for s in range(SHIFTS):
            line = jnp.broadcast_to(profile[s : s + 1], (LANES, wide))
            rolled = pltpu.roll(line, 0, 1, stride=1, stride_axis=0)
            table_ref[s * LANES : (s + 1) * LANES, :] = jnp.where(inside, rolled, 0.0).astype(
                jnp.bfloat16
            )


def build_tables(basis_rows, basis_cols, visit_coeff, new_coeff):
    table = jax.ShapeDtypeStruct((SHIFTS * LANES, QUAD * SPLIT), jnp.bfloat16)
    return pl.pallas_call(
        table_kernel,
        out_shape=(table, table),
        compiler_params=params(),
        cost_estimate=pl.CostEstimate(flops=10**9, bytes_accessed=4 * 10**6, transcendentals=0),
        name="tables",
    )(basis_rows.T, basis_cols.T, visit_coeff, new_coeff)


def split_shift(shift):
    turn = lax.rem(shift + 2 * LANES, LANES)
    return turn, (turn - shift) // LANES


def moved_block(load, blocks, h, shift, lane):
    turn, back = split_shift(shift)

    def block(j):
        clamped = jnp.clip(j, 0, blocks - 1)
        return jnp.where(clamped == j, load(clamped), 0)

    joined = jnp.where(lane < LANES - turn, block(h + back), block(h + back - 1))
    return pltpu.roll(joined, turn, 1)


def cover_kernel(offset_ref, weight_ref, mask_ref, out_ref, lines):
    height, columns = mask_ref.shape
    blocks = columns // LANES
    offset = offset_ref[0]
    weight = weight_ref[0]
    count = 32
    lane = lax.broadcasted_iota(jnp.int32, (count, LANES), 1)

    def body(c, carry):
        first = pl.multiple_of(c * count, count)

        def load(j):
            return mask_ref[pl.ds(first, count), pl.ds(pl.multiple_of(j * LANES, LANES), LANES)]

        for h in range(blocks):
            good = moved_block(load, blocks, h, offset, lane)
            lines[pl.ds(h, count, stride=blocks), :] = weight * good.astype(jnp.float32)
        out_ref[pl.ds(first, count)] = (
            lines[...].reshape(count, blocks, LANES).astype(jnp.bfloat16)
        )
        return carry

    lax.fori_loop(0, height // count, body, 0)


def cover_rows(offset, weight, mask):
    height, columns = mask.shape
    blocks = columns // LANES
    smem = pl.BlockSpec(memory_space=pltpu.SMEM)
    vmem = pl.BlockSpec(memory_space=pltpu.VMEM)
    return pl.pallas_call(
        cover_kernel,
        out_shape=jax.ShapeDtypeStruct((height, blocks, LANES), jnp.bfloat16),
        in_specs=[smem, smem, vmem],
        out_specs=vmem,
        scratch_shapes=[pltpu.VMEM((32 * blocks, LANES), jnp.float32)],
        compiler_params=params(),
        name="cover_rows",
    )(offset, weight, mask)


def multiply(windows, table_ref, first, write):
    quads = CHUNK // QUAD
    parts = []
    for s in range(SHIFTS):
        start = s + HALO - HALF
        part = windows[pl.ds(first // QUAD + start // QUAD, quads), start % QUAD]
        parts.append(part.reshape(-1, LANES))
    product = jnp.dot(
        jnp.concatenate(parts, axis=1), table_ref[...], preferred_element_type=jnp.float32
    )
    blocks = windows.shape[2] // 2
    lane = lax.broadcasted_iota(jnp.int32, (blocks, LANES), 1)
    for q in range(quads):
        for pair in range(QUAD // 2):
            lanes = slice(pair * LANES, (pair + 1) * LANES)
            a = product[(2 * q) * blocks : (2 * q + 1) * blocks, lanes]
            b = product[(2 * q + 1) * blocks : (2 * q + 2) * blocks, lanes]
            crossed = pltpu.roll(jnp.where(lane < SPLIT, b, a), SPLIT, 1)
            row = q * QUAD + 2 * pair
            write(row, jnp.where(lane < SPLIT, a, crossed))
            write(row + 1, jnp.where(lane < SPLIT, crossed, b))


def visit_kernel(
    offset_ref, weight_ref, low_ref, mid_ref, high_ref, cover_ref, table_ref, out_ref, lines, windows
):
    weight = weight_ref[0]
    height, columns = mid_ref.shape
    blocks = columns // LANES
    shift = offset_ref[0] + HALF
    lane = lax.broadcasted_iota(jnp.int32, (HALO, LANES), 1)

    def fill(source, first, row):
        def load(j):
            return source[
                pl.ds(first, HALO), pl.ds(pl.multiple_of(j * LANES, LANES), LANES)
            ].astype(jnp.float32)

        for align in range(2):
            for h in range(blocks):
                lines[pl.ds(align * blocks + h, HALO, stride=2 * blocks), :] = moved_block(
                    load, blocks, h, shift - align * SPLIT, lane
                )
        windows[pl.ds(row // QUAD, HALO // QUAD)] = (
            lines[...].reshape(HALO // QUAD, QUAD, 2 * blocks, LANES).astype(jnp.bfloat16)
        )

    fill(low_ref, 0, 0)

    def body(c, carry):
        first = pl.multiple_of(c * HALO, HALO)
        fill(mid_ref, first, first + HALO)
        return carry

    lax.fori_loop(0, height // HALO, body, 0)
    fill(high_ref, 0, HALO + height)

    def chunk(c, carry):
        first = pl.multiple_of(c * CHUNK, CHUNK)

        def write(row, line):
            good = cover_ref[first + row].astype(jnp.float32) > 0
            out_ref[first + row] = (line * jnp.where(good, weight, 0.0)).astype(jnp.bfloat16)

        multiply(windows, table_ref, first, write)
        return carry

    lax.fori_loop(0, height // CHUNK, chunk, 0)


def window_scratch(height, blocks):
    return pltpu.VMEM(((height + 2 * HALO) // QUAD, QUAD, 2 * blocks, LANES), jnp.bfloat16)


def conv_cost(height, columns):
    return pl.CostEstimate(
        flops=2 * height * columns * SHIFTS * LANES, bytes_accessed=8 * 10**6, transcendentals=0
    )


def match_visit(low, mid, high, cover, table, offset, weight):
    height, columns = mid.shape
    blocks = columns // LANES
    smem = pl.BlockSpec(memory_space=pltpu.SMEM)
    vmem = pl.BlockSpec(memory_space=pltpu.VMEM)
    return pl.pallas_call(
        visit_kernel,
        out_shape=jax.ShapeDtypeStruct(cover.shape, jnp.bfloat16),
        in_specs=[smem, smem] + [vmem] * 5,
        out_specs=vmem,
        scratch_shapes=[
            pltpu.VMEM((HALO * 2 * blocks, LANES), jnp.float32),
            window_scratch(height, blocks),
        ],
        compiler_params=params(),
        cost_estimate=conv_cost(height, columns),
        name="match_visit",
    )(offset, weight, low, mid, high, cover, table)


def new_kernel(low_ref, mid_ref, high_ref, new_ref, table_ref, out_ref, padded, windows, lines):
    height, blocks, _ = mid_ref.shape
    edge = jnp.zeros((HALO, 8, LANES), jnp.float32)
    padded[:, :8] = edge
    padded[:, 8 + blocks :] = edge
    lane = lax.broadcasted_iota(jnp.int32, (HALO, blocks, LANES), 2)
    turn = SPLIT + HALF

    def fill(source, first, row):
        here = source[pl.ds(first, HALO)].astype(jnp.float32)
        padded[:, 8 : 8 + blocks] = here
        before = padded[:, 7 : 7 + blocks]
        after = padded[:, 9 : 9 + blocks]
        left = pltpu.roll(jnp.where(lane < LANES - HALF, here, before), HALF, 2)
        right = pltpu.roll(jnp.where(lane < LANES - turn, after, here), turn, 2)
        both = jnp.concatenate([left, right], axis=1).astype(jnp.bfloat16)
        windows[pl.ds(row // QUAD, HALO // QUAD)] = both.reshape(
            HALO // QUAD, QUAD, 2 * blocks, LANES
        )

    fill(low_ref, 0, 0)

    def body(c, carry):
        first = pl.multiple_of(c * HALO, HALO)
        fill(mid_ref, first, first + HALO)
        return carry

    lax.fori_loop(0, height // HALO, body, 0)
    fill(high_ref, 0, HALO + height)

    def chunk(c, carry):
        first = pl.multiple_of(c * CHUNK, CHUNK)

        def write(row, line):
            lines[row * blocks : (row + 1) * blocks, :] = line

        multiply(windows, table_ref, first, write)
        for h in range(blocks):
            lanes = slice(h * LANES, (h + 1) * LANES)
            out_ref[pl.ds(first, CHUNK), lanes] = (
                new_ref[pl.ds(first, CHUNK), lanes].astype(jnp.float32)
                - lines[pl.ds(h, CHUNK, stride=blocks), :]
            )
        return carry

    lax.fori_loop(0, height // CHUNK, chunk, 0)


def subtract(low, mid, high, new, table):
    height, blocks, _ = mid.shape
    vmem = pl.BlockSpec(memory_space=pltpu.VMEM)
    return pl.pallas_call(
        new_kernel,
        out_shape=jax.ShapeDtypeStruct(new.shape, jnp.float32),
        in_specs=[vmem] * 5,
        out_specs=vmem,
        scratch_shapes=[
            pltpu.VMEM((HALO, blocks + 16, LANES), jnp.float32),
            window_scratch(height, blocks),
            pltpu.VMEM((CHUNK * blocks, LANES), jnp.float32),
        ],
        compiler_params=params(),
        cost_estimate=conv_cost(*new.shape),
        name="subtract",
    )(low, mid, high, new, table)


def sum_kernel(patch_ref, received_ref, sums):
    sums[...] = jnp.zeros_like(sums)

    def add(v, carry):
        p = patch_ref[v]
        sums[p] = sums[p] + received_ref[v].astype(jnp.float32)
        return carry

    lax.fori_loop(0, received_ref.shape[0], add, 0)


def sum_cover(received, patch_of):
    smem = pl.BlockSpec(memory_space=pltpu.SMEM)
    vmem = pl.BlockSpec(memory_space=pltpu.VMEM)
    return pl.pallas_call(
        sum_kernel,
        out_shape=jax.ShapeDtypeStruct((PATCHES,) + received.shape[1:], jnp.float32),
        in_specs=[smem, vmem],
        out_specs=vmem,
        compiler_params=params(),
        name="sum_cover",
    )(patch_of, received)


def combine_kernel(patch_ref, wanted_ref, received_ref, cover_ref, coadd_ref, send_ref, sums, packed, lines):
    sum_kernel(patch_ref, received_ref, sums)
    _, rows, blocks, _ = sums.shape
    for p in range(PATCHES):
        ratio = sums[p] / jnp.maximum(cover_ref[p], 1.0)
        packed[p] = ratio.astype(jnp.bfloat16)
        lines[...] = ratio.reshape(rows * blocks, LANES)
        for h in range(blocks):
            coadd_ref[p, :, h * LANES : (h + 1) * LANES] = lines[
                pl.ds(h, rows, stride=blocks), :
            ].astype(jnp.bfloat16)

    def place(n, carry):
        send_ref[n] = packed[wanted_ref[n]]
        return carry

    lax.fori_loop(0, send_ref.shape[0], place, 0)


def combine(received, cover, patch_of, new_patch):
    visits, rows, blocks, _ = received.shape
    smem = pl.BlockSpec(memory_space=pltpu.SMEM)
    vmem = pl.BlockSpec(memory_space=pltpu.VMEM)
    return pl.pallas_call(
        combine_kernel,
        out_shape=(
            jax.ShapeDtypeStruct((PATCHES, rows, blocks * LANES), jnp.bfloat16),
            jax.ShapeDtypeStruct((new_patch.shape[0],) + received.shape[1:], jnp.bfloat16),
        ),
        in_specs=[smem, smem, vmem, vmem],
        out_specs=(vmem, vmem),
        scratch_shapes=[
            pltpu.VMEM((PATCHES, rows, blocks, LANES), jnp.float32),
            pltpu.VMEM((PATCHES, rows, blocks, LANES), jnp.bfloat16),
            pltpu.VMEM((rows * blocks, LANES), jnp.float32),
        ],
        compiler_params=params(),
        name="combine",
    )(patch_of, new_patch, received, cover)


def to_owners(lines):
    height, blocks, _ = lines.shape
    owners = lax.axis_size("visit")
    return lax.all_to_all(
        lines.reshape(owners, height // owners, blocks, LANES),
        "visit",
        split_axis=0,
        concat_axis=0,
        tiled=True,
    )


def per_device(
    visit_image,
    good_mask,
    basis_rows,
    basis_cols,
    visit_coeff,
    visit_weight,
    col_offset,
    patch_of,
    new_image,
    new_coeff,
    new_patch,
):
    cover = cover_rows(col_offset, visit_weight, good_mask[0])
    received_cover = to_owners(cover)
    low, high = neighbours(visit_image[0], "tile")
    visit_table, new_table = build_tables(basis_rows, basis_cols, visit_coeff, new_coeff)
    weighted = match_visit(
        low, visit_image[0], high, cover, visit_table, col_offset, visit_weight
    )
    received = to_owners(weighted)
    cover_sums = sum_cover(received_cover, patch_of[:, 0])
    coadd, wanted = combine(received, cover_sums, patch_of[:, 0], new_patch[:, 0])
    template = lax.all_to_all(wanted, "visit", split_axis=0, concat_axis=0, tiled=True)
    template = template.reshape((-1,) + template.shape[2:])
    low, high = neighbours(template, "tile")
    difference = subtract(low, template, high, new_image[0], new_table)
    return (coadd[:, None], difference[None])


def solution(mesh):
    return jax.shard_map(
        per_device,
        mesh=mesh,
        in_specs=(
            P("visit", "tile", None),
            P("visit", "tile", None),
            P(),
            P(),
            P("visit", None),
            P("visit"),
            P("visit"),
            P(),
            P("visit", "tile", None),
            P("visit", None),
            P(),
        ),
        out_specs=(P(None, "tile", "visit", None), P("visit", "tile", None)),
        check_vma=False,
    )
```

```python
import jax
import jax.numpy as jnp
from jax import lax
from jax.experimental import pallas as pl
from jax.experimental.pallas import tpu as pltpu
from jax.sharding import PartitionSpec as P

KS = 21
HALF = KS // 2
PATCHES = 8
LANES = 128
HALO = 16
QUAD = 4
SPLIT = LANES // 2
SHIFTS = QUAD + KS - 1
CHUNK = 64
PARTS = 4
UNIT = 16
PAD = 8
VMEM_LIMIT = 24 * 2**20


def params():
    return pltpu.CompilerParams(vmem_limit_bytes=VMEM_LIMIT)


def neighbours(block, axis):
    count = lax.axis_size(axis)
    forward = [(i, i + 1) for i in range(count - 1)]
    backward = [(target, source) for source, target in forward]
    low = lax.ppermute(block[-HALO:], axis, forward)
    high = lax.ppermute(block[:HALO], axis, backward)
    return low, high


def table_kernel(rows_ref, cols_ref, first_ref, second_ref, *table_refs):
    wide = QUAD * SPLIT
    tap = lax.broadcasted_iota(jnp.int32, (KS, wide), 0)
    place = lax.broadcasted_iota(jnp.int32, (KS, wide), 1)
    shift = lax.broadcasted_iota(jnp.int32, (SHIFTS, KS), 0)
    row_tap = lax.broadcasted_iota(jnp.int32, (SHIFTS, KS), 1)
    lane = lax.broadcasted_iota(jnp.int32, (LANES, wide), 0)
    column = lax.broadcasted_iota(jnp.int32, (LANES, wide), 1) % SPLIT
    inside = (lane >= column) & (lane - column < KS)
    for coeff_ref, table_ref in zip((first_ref, second_ref), table_refs):
        kernel = lax.dot_general(
            rows_ref[...] * coeff_ref[...],
            cols_ref[...],
            (((1,), (1,)), ((), ())),
            precision=lax.Precision.HIGHEST,
            preferred_element_type=jnp.float32,
        ).astype(jnp.bfloat16)
        profile = jnp.zeros((SHIFTS, wide), jnp.float32)
        for e in range(QUAD):
            at = (SPLIT * e - tap) % wide
            spread = jnp.dot(
                kernel, (place == at).astype(jnp.bfloat16), preferred_element_type=jnp.float32
            )
            lowered = (shift - e == row_tap).astype(jnp.bfloat16)
            profile = profile + jnp.dot(
                lowered, spread.astype(jnp.bfloat16), preferred_element_type=jnp.float32
            )
        for s in range(SHIFTS):
            line = jnp.broadcast_to(profile[s : s + 1], (LANES, wide))
            rolled = pltpu.roll(line, 0, 1, stride=1, stride_axis=0)
            table_ref[s * LANES : (s + 1) * LANES, :] = jnp.where(inside, rolled, 0.0).astype(
                jnp.bfloat16
            )


def build_tables(basis_rows, basis_cols, visit_coeff, new_coeff):
    table = jax.ShapeDtypeStruct((SHIFTS * LANES, QUAD * SPLIT), jnp.bfloat16)
    return pl.pallas_call(
        table_kernel,
        out_shape=(table, table),
        compiler_params=params(),
        cost_estimate=pl.CostEstimate(flops=10**9, bytes_accessed=4 * 10**6, transcendentals=0),
        name="tables",
    )(basis_rows.T, basis_cols.T, visit_coeff, new_coeff)


def split_shift(shift):
    turn = lax.rem(shift + 2 * LANES, LANES)
    return turn, (turn - shift) // LANES


def lay_out(blocks_of, shift, lines, base, pitch):
    turn, back = split_shift(shift)
    count = blocks_of[0].shape[0]
    lane = lax.broadcasted_iota(jnp.int32, (count, LANES), 1)
    before = jnp.zeros((count, LANES), blocks_of[0].dtype)
    for k in range(len(blocks_of) + 1):
        here = pltpu.roll(blocks_of[k], turn, 1) if k < len(blocks_of) else jnp.zeros_like(before)
        lines[pl.ds(base + k - back, count, stride=pitch), :] = jnp.where(
            lane >= turn, here, before
        )
        before = here


def lanes_of(h):
    return slice(h * LANES, (h + 1) * LANES)


def cover_kernel(offset_ref, weight_ref, mask_ref, out_ref, *lines):
    height, columns = mask_ref.shape
    blocks = columns // LANES
    weight = weight_ref[0]
    for u in range(height // UNIT):
        spot = lines[u % len(lines)]
        rows = slice(u * UNIT, (u + 1) * UNIT)
        good = [mask_ref[rows, lanes_of(h)].astype(jnp.float32) * weight for h in range(blocks)]
        lay_out(good, offset_ref[0], spot, PAD, 2 * blocks)
        tiles = spot[...].reshape(UNIT, 2 * blocks, LANES)
        out_ref[rows] = tiles[:, PAD : PAD + blocks].astype(jnp.bfloat16)


def cover_rows(offset, weight, mask):
    height, columns = mask.shape
    blocks = columns // LANES
    smem = pl.BlockSpec(memory_space=pltpu.SMEM)
    vmem = pl.BlockSpec(memory_space=pltpu.VMEM)
    return pl.pallas_call(
        cover_kernel,
        out_shape=jax.ShapeDtypeStruct((height, blocks, LANES), jnp.bfloat16),
        in_specs=[smem, smem, vmem],
        out_specs=vmem,
        scratch_shapes=[pltpu.VMEM((UNIT * 2 * blocks, LANES), jnp.float32)] * 4,
        compiler_params=params(),
        cost_estimate=pl.CostEstimate(flops=10**6, bytes_accessed=6 * 10**6, transcendentals=0),
        name="cover_rows",
    )(offset, weight, mask)


def multiply(windows, starts, table_ref, write):
    parts = []
    for s in range(SHIFTS):
        at = s + HALO - HALF
        pieces = [
            windows[first + at // QUAD : first + at // QUAD + count, at % QUAD]
            for first, count in starts
        ]
        part = pieces[0] if len(pieces) == 1 else jnp.concatenate(pieces, axis=0)
        parts.append(part.reshape(-1, LANES))
    product = jnp.dot(
        jnp.concatenate(parts, axis=1), table_ref[...], preferred_element_type=jnp.float32
    )
    blocks = windows.shape[2] // 2
    lane = lax.broadcasted_iota(jnp.int32, (blocks, LANES), 1)
    for k in range(sum(count for _, count in starts)):
        for pair in range(QUAD // 2):
            a = product[(2 * k) * blocks : (2 * k + 1) * blocks, lanes_of(pair)]
            b = product[(2 * k + 1) * blocks : (2 * k + 2) * blocks, lanes_of(pair)]
            crossed = pltpu.roll(jnp.where(lane < SPLIT, b, a), SPLIT, 1)
            write(k, 2 * pair, jnp.where(lane < SPLIT, a, crossed))
            write(k, 2 * pair + 1, jnp.where(lane < SPLIT, crossed, b))


def visit_kernel(
    offset_ref, weight_ref, low_ref, mid_ref, high_ref, cover_ref, table_ref, out_ref, windows, *lines
):
    weight = weight_ref[0]
    height, columns = mid_ref.shape
    blocks = columns // LANES
    shift = offset_ref[0] + HALF
    rows = out_ref.shape[2]
    pitch = 4 * blocks

    def fill(u):
        spot = lines[u % len(lines)]
        if u == 0:
            source, at = low_ref, slice(0, UNIT)
        elif u == height // UNIT + 1:
            source, at = high_ref, slice(0, UNIT)
        else:
            source, at = mid_ref, slice((u - 1) * UNIT, u * UNIT)
        pixels = [source[at, lanes_of(h)].astype(jnp.float32) for h in range(blocks)]
        lay_out(pixels, shift, spot, PAD, pitch)
        lay_out(pixels, shift - SPLIT, spot, PAD + 2 * blocks, pitch)
        tiles = spot[...].reshape(UNIT, pitch, LANES)
        both = [tiles[:, PAD + 2 * blocks * k : PAD + 2 * blocks * k + blocks] for k in range(2)]
        windows[u * (UNIT // QUAD) : (u + 1) * (UNIT // QUAD)] = (
            jnp.concatenate(both, axis=1)
            .astype(jnp.bfloat16)
            .reshape(UNIT // QUAD, QUAD, 2 * blocks, LANES)
        )

    done = 0
    for first in range(0, height, CHUNK):
        needed = min((first + CHUNK + 2 * HALO) // UNIT, height // UNIT + 2)
        for u in range(done, needed):
            fill(u)
        done = needed

        def write(k, e, line, first=first):
            r = first + QUAD * k + e
            cover = cover_ref[r]
            good = cover.astype(jnp.float32) > 0
            out_ref[r // rows, 0, r % rows] = (line * jnp.where(good, weight, 0.0)).astype(
                jnp.bfloat16
            )
            out_ref[r // rows, 1, r % rows] = cover

        multiply(windows, [(first // QUAD, CHUNK // QUAD)], table_ref, write)


def window_scratch(height, blocks):
    return pltpu.VMEM((height // QUAD, QUAD, 2 * blocks, LANES), jnp.bfloat16)


def conv_cost(height, columns):
    return pl.CostEstimate(
        flops=2 * height * columns * SHIFTS * LANES, bytes_accessed=8 * 10**6, transcendentals=0
    )


def match_visit(low, mid, high, cover, table, offset, weight, owners):
    height, columns = mid.shape
    blocks = columns // LANES
    smem = pl.BlockSpec(memory_space=pltpu.SMEM)
    vmem = pl.BlockSpec(memory_space=pltpu.VMEM)
    return pl.pallas_call(
        visit_kernel,
        out_shape=jax.ShapeDtypeStruct(
            (owners, 2, height // owners, blocks, LANES), jnp.bfloat16
        ),
        in_specs=[smem, smem] + [vmem] * 5,
        out_specs=vmem,
        scratch_shapes=[window_scratch(height + 2 * HALO, blocks)]
        + [pltpu.VMEM((UNIT * 4 * blocks, LANES), jnp.float32)] * 4,
        compiler_params=params(),
        cost_estimate=conv_cost(height, columns),
        name="match_visit",
    )(offset, weight, low, mid, high, cover, table)


def fill_windows(source, first, padded, windows, unit):
    blocks = source.shape[1]
    turn = SPLIT + HALF
    lane = lax.broadcasted_iota(jnp.int32, (UNIT, blocks, LANES), 2)
    here = source[first : first + UNIT].astype(jnp.float32)
    padded[:, PAD : PAD + blocks] = here
    before = padded[:, PAD - 1 : PAD - 1 + blocks]
    after = padded[:, PAD + 1 : PAD + 1 + blocks]
    left = pltpu.roll(jnp.where(lane < LANES - HALF, here, before), HALF, 2)
    right = pltpu.roll(jnp.where(lane < LANES - turn, after, here), turn, 2)
    both = jnp.concatenate([left, right], axis=1).astype(jnp.bfloat16)
    windows[unit * (UNIT // QUAD) : (unit + 1) * (UNIT // QUAD)] = both.reshape(
        UNIT // QUAD, QUAD, 2 * blocks, LANES
    )


def zero_edges(padded, blocks):
    edge = jnp.zeros((UNIT, PAD, LANES), jnp.float32)
    for spot in padded:
        spot[:, :PAD] = edge
        spot[:, PAD + blocks :] = edge


def interior_kernel(mid_ref, new_ref, table_ref, out_ref, windows, result, lines, sems, *padded):
    height, blocks, _ = mid_ref.shape
    zero_edges(padded, blocks)
    rows = (height - 2 * HALO) // PARTS
    copies = []
    done = 0
    for part in range(PARTS):
        first = HALO + part * rows
        needed = -(-(first + rows + HALF + 1) // UNIT)
        for u in range(done, min(needed, height // UNIT)):
            fill_windows(mid_ref, u * UNIT, padded[u % len(padded)], windows, u + 1)
        done = needed
        spot = lines.at[part % 2]

        def write(k, e, line, spot=spot):
            row = QUAD * k + e
            spot[row * blocks : (row + 1) * blocks, :] = line

        multiply(windows, [(first // QUAD, rows // QUAD)], table_ref, write)
        for h in range(blocks):
            result[first - HALO : first - HALO + rows, lanes_of(h)] = (
                new_ref[first : first + rows, lanes_of(h)].astype(jnp.float32)
                - spot[pl.ds(h, rows, stride=blocks), :]
            )
        copy = pltpu.make_async_copy(
            result.at[pl.ds(first - HALO, rows)], out_ref.at[pl.ds(first, rows)], sems.at[part]
        )
        copy.start()
        copies.append(copy)
    for copy in copies:
        copy.wait()


def subtract_interior(mid, new, table):
    height, blocks, _ = mid.shape
    vmem = pl.BlockSpec(memory_space=pltpu.VMEM)
    rows = (height - 2 * HALO) // PARTS
    return pl.pallas_call(
        interior_kernel,
        out_shape=jax.ShapeDtypeStruct(new.shape, jnp.float32),
        in_specs=[vmem] * 3,
        out_specs=pl.BlockSpec(memory_space=pl.ANY),
        scratch_shapes=[
            window_scratch(height + 2 * HALO, blocks),
            pltpu.VMEM((height - 2 * HALO, blocks * LANES), jnp.float32),
            pltpu.VMEM((2, rows * blocks, LANES), jnp.float32),
            pltpu.SemaphoreType.DMA((PARTS,)),
        ]
        + [pltpu.VMEM((UNIT, blocks + 2 * PAD, LANES), jnp.float32)] * 4,
        compiler_params=params(),
        cost_estimate=conv_cost(*new.shape),
        name="subtract_interior",
    )(mid, new, table)


def edge_kernel(low_ref, mid_ref, high_ref, new_ref, table_ref, _, out_ref, windows, result, lines, sems, *padded):
    height, blocks, _ = mid_ref.shape
    zero_edges(padded, blocks)
    sources = [
        (low_ref, 0),
        (mid_ref, 0),
        (mid_ref, UNIT),
        (mid_ref, height - 2 * UNIT),
        (mid_ref, height - UNIT),
        (high_ref, 0),
    ]
    for u, (source, first) in enumerate(sources):
        fill_windows(source, first, padded[u % len(padded)], windows, u)

    def write(k, e, line):
        row = QUAD * k + e
        lines[row * blocks : (row + 1) * blocks, :] = line

    each = HALO // QUAD
    multiply(windows, [(0, each), (3 * UNIT // QUAD, each)], table_ref, write)
    copies = []
    for side, first in enumerate((0, height - HALO)):
        for h in range(blocks):
            result[side, :, lanes_of(h)] = (
                new_ref[first : first + HALO, lanes_of(h)].astype(jnp.float32)
                - lines[pl.ds(side * HALO * blocks + h, HALO, stride=blocks), :]
            )
        copy = pltpu.make_async_copy(
            result.at[side], out_ref.at[pl.ds(first, HALO)], sems.at[side]
        )
        copy.start()
        copies.append(copy)
    for copy in copies:
        copy.wait()


def subtract_edges(low, mid, high, new, table, difference):
    _, blocks, _ = mid.shape
    vmem = pl.BlockSpec(memory_space=pltpu.VMEM)
    return pl.pallas_call(
        edge_kernel,
        out_shape=jax.ShapeDtypeStruct(difference.shape, difference.dtype),
        in_specs=[vmem] * 5 + [pl.BlockSpec(memory_space=pl.ANY)],
        out_specs=pl.BlockSpec(memory_space=pl.ANY),
        input_output_aliases={5: 0},
        scratch_shapes=[
            window_scratch(6 * UNIT, blocks),
            pltpu.VMEM((2, HALO, blocks * LANES), jnp.float32),
            pltpu.VMEM((2 * HALO * blocks, LANES), jnp.float32),
            pltpu.SemaphoreType.DMA((2,)),
        ]
        + [pltpu.VMEM((UNIT, blocks + 2 * PAD, LANES), jnp.float32)] * 3,
        compiler_params=params(),
        cost_estimate=conv_cost(2 * HALO, new.shape[1]),
        name="subtract_edges",
    )(low, mid, high, new, table, difference)


def combine_kernel(patch_ref, wanted_ref, received_ref, coadd_ref, send_ref, sums, packed, lines):
    _, _, rows, blocks, _ = received_ref.shape
    sums[...] = jnp.zeros_like(sums)

    def add(v, carry):
        p = patch_ref[v]
        sums[p] = sums[p] + received_ref[v].astype(jnp.float32)
        return carry

    lax.fori_loop(0, received_ref.shape[0], add, 0)
    for p in range(PATCHES):
        ratio = sums[p, 0] / jnp.maximum(sums[p, 1], 1.0)
        packed[p] = ratio.astype(jnp.bfloat16)
        lines[p] = ratio.reshape(rows * blocks, LANES)
        for h in range(blocks):
            coadd_ref[p, :, lanes_of(h)] = lines[p, pl.ds(h, rows, stride=blocks), :].astype(
                jnp.bfloat16
            )

    def place(n, carry):
        send_ref[n] = packed[wanted_ref[n]]
        return carry

    lax.fori_loop(0, send_ref.shape[0], place, 0)


def combine(received, patch_of, new_patch):
    _, _, rows, blocks, _ = received.shape
    smem = pl.BlockSpec(memory_space=pltpu.SMEM)
    vmem = pl.BlockSpec(memory_space=pltpu.VMEM)
    return pl.pallas_call(
        combine_kernel,
        out_shape=(
            jax.ShapeDtypeStruct((PATCHES, rows, blocks * LANES), jnp.bfloat16),
            jax.ShapeDtypeStruct((new_patch.shape[0], rows, blocks, LANES), jnp.bfloat16),
        ),
        in_specs=[smem, smem, vmem],
        out_specs=(vmem, vmem),
        scratch_shapes=[
            pltpu.VMEM((PATCHES, 2, rows, blocks, LANES), jnp.float32),
            pltpu.VMEM((PATCHES, rows, blocks, LANES), jnp.bfloat16),
            pltpu.VMEM((PATCHES, rows * blocks, LANES), jnp.float32),
        ],
        compiler_params=params(),
        name="combine",
    )(patch_of, new_patch, received)


def exchange(chunks):
    return lax.all_to_all(chunks, "visit", split_axis=0, concat_axis=0, tiled=True)


def per_device(
    visit_image,
    good_mask,
    basis_rows,
    basis_cols,
    visit_coeff,
    visit_weight,
    col_offset,
    patch_of,
    new_image,
    new_coeff,
    new_patch,
):
    owners = lax.axis_size("visit")
    low, high = neighbours(visit_image[0], "tile")
    visit_table, new_table = build_tables(basis_rows, basis_cols, visit_coeff, new_coeff)
    cover = cover_rows(col_offset, visit_weight, good_mask[0])
    outgoing = match_visit(
        low, visit_image[0], high, cover, visit_table, col_offset, visit_weight, owners
    )
    received = exchange(outgoing)
    coadd, wanted = combine(received, patch_of[:, 0], new_patch[:, 0])
    template = exchange(wanted)
    template = template.reshape((-1,) + template.shape[2:])
    low, high = neighbours(template, "tile")
    difference = subtract_interior(template, new_image[0], new_table)
    difference = subtract_edges(low, template, high, new_image[0], new_table, difference)
    return (coadd[:, None], difference[None])


def solution(mesh):
    return jax.shard_map(
        per_device,
        mesh=mesh,
        in_specs=(
            P("visit", "tile", None),
            P("visit", "tile", None),
            P(),
            P(),
            P("visit", None),
            P("visit"),
            P("visit"),
            P(),
            P("visit", "tile", None),
            P("visit", None),
            P(),
        ),
        out_specs=(P(None, "tile", "visit", None), P("visit", "tile", None)),
        check_vma=False,
    )
```

```python
import jax
import jax.numpy as jnp
from jax import lax
from jax.experimental import pallas as pl
from jax.experimental.pallas import tpu as pltpu
from jax.sharding import PartitionSpec as P

KS = 21
HALF = KS // 2
PATCHES = 8
LANES = 128
HALO = 16
QUAD = 4
SPLIT = LANES // 2
SHIFTS = QUAD + KS - 1
PARTS = 4
UNIT = 16
PAD = 8
VMEM_LIMIT = 16 * 2**20


def params():
    return pltpu.CompilerParams(vmem_limit_bytes=VMEM_LIMIT)


def neighbours(block, axis):
    count = lax.axis_size(axis)
    forward = [(i, i + 1) for i in range(count - 1)]
    backward = [(target, source) for source, target in forward]
    low = lax.ppermute(block[-HALO:], axis, forward)
    high = lax.ppermute(block[:HALO], axis, backward)
    return low, high


def fill_table(rows_ref, cols_ref, coeff_ref, table_ref):
    wide = QUAD * SPLIT
    tap = lax.broadcasted_iota(jnp.int32, (KS, wide), 0)
    place = lax.broadcasted_iota(jnp.int32, (KS, wide), 1)
    shift = lax.broadcasted_iota(jnp.int32, (SHIFTS, KS), 0)
    row_tap = lax.broadcasted_iota(jnp.int32, (SHIFTS, KS), 1)
    lane = lax.broadcasted_iota(jnp.int32, (LANES, wide), 0)
    column = lax.broadcasted_iota(jnp.int32, (LANES, wide), 1) % SPLIT
    inside = (lane >= column) & (lane - column < KS)
    kernel = lax.dot_general(
        rows_ref[...] * coeff_ref[...],
        cols_ref[...],
        (((1,), (1,)), ((), ())),
        precision=lax.Precision.HIGHEST,
        preferred_element_type=jnp.float32,
    ).astype(jnp.bfloat16)
    profile = jnp.zeros((SHIFTS, wide), jnp.float32)
    for e in range(QUAD):
        at = (SPLIT * e - tap) % wide
        spread = jnp.dot(
            kernel, (place == at).astype(jnp.bfloat16), preferred_element_type=jnp.float32
        )
        lowered = (shift - e == row_tap).astype(jnp.bfloat16)
        profile = profile + jnp.dot(
            lowered, spread.astype(jnp.bfloat16), preferred_element_type=jnp.float32
        )
    for s in range(SHIFTS):
        line = jnp.broadcast_to(profile[s : s + 1], (LANES, wide))
        rolled = pltpu.roll(line, 0, 1, stride=1, stride_axis=0)
        table_ref[s * LANES : (s + 1) * LANES, :] = jnp.where(inside, rolled, 0.0).astype(
            jnp.bfloat16
        )


def build_table(basis_rows, basis_cols, coeff):
    return pl.pallas_call(
        fill_table,
        out_shape=jax.ShapeDtypeStruct((SHIFTS * LANES, QUAD * SPLIT), jnp.bfloat16),
        compiler_params=params(),
        cost_estimate=pl.CostEstimate(flops=10**9, bytes_accessed=2 * 10**6, transcendentals=0),
        name="table",
    )(basis_rows.T, basis_cols.T, coeff)


def split_shift(shift):
    turn = lax.rem(shift + 2 * LANES, LANES)
    return turn, (turn - shift) // LANES


def lay_out(blocks_of, shift, lines, base, pitch):
    turn, back = split_shift(shift)
    count = blocks_of[0].shape[0]
    lane = lax.broadcasted_iota(jnp.int32, (count, LANES), 1)
    before = jnp.zeros((count, LANES), blocks_of[0].dtype)
    for k in range(len(blocks_of) + 1):
        here = pltpu.roll(blocks_of[k], turn, 1) if k < len(blocks_of) else jnp.zeros_like(before)
        lines[pl.ds(base + k - back, count, stride=pitch), :] = jnp.where(
            lane >= turn, here, before
        )
        before = here


def lanes_of(h):
    return slice(h * LANES, (h + 1) * LANES)


def multiply(windows, starts, table_ref, write):
    parts = []
    for s in range(SHIFTS):
        at = s + HALO - HALF
        pieces = [
            windows[first + at // QUAD : first + at // QUAD + count, at % QUAD]
            for first, count in starts
        ]
        part = pieces[0] if len(pieces) == 1 else jnp.concatenate(pieces, axis=0)
        parts.append(part.reshape(-1, LANES))
    product = jnp.dot(
        jnp.concatenate(parts, axis=1), table_ref[...], preferred_element_type=jnp.float32
    )
    blocks = windows.shape[2] // 2
    lane = lax.broadcasted_iota(jnp.int32, (blocks, LANES), 1)
    for k in range(sum(count for _, count in starts)):
        for pair in range(QUAD // 2):
            a = product[(2 * k) * blocks : (2 * k + 1) * blocks, lanes_of(pair)]
            b = product[(2 * k + 1) * blocks : (2 * k + 2) * blocks, lanes_of(pair)]
            crossed = pltpu.roll(jnp.where(lane < SPLIT, b, a), SPLIT, 1)
            write(k, 2 * pair, jnp.where(lane < SPLIT, a, crossed))
            write(k, 2 * pair + 1, jnp.where(lane < SPLIT, crossed, b))


def lay_out_unit(source, first, shift, spot, windows, unit):
    blocks = windows.shape[2] // 2
    pitch = 4 * blocks
    pixels = [source[first : first + UNIT, lanes_of(h)].astype(jnp.float32) for h in range(blocks)]
    lay_out(pixels, shift, spot, PAD, pitch)
    lay_out(pixels, shift - SPLIT, spot, PAD + 2 * blocks, pitch)
    tiles = spot[...].reshape(UNIT, pitch, LANES)
    both = [tiles[:, PAD + 2 * blocks * k : PAD + 2 * blocks * k + blocks] for k in range(2)]
    windows[unit * (UNIT // QUAD) : (unit + 1) * (UNIT // QUAD)] = (
        jnp.concatenate(both, axis=1)
        .astype(jnp.bfloat16)
        .reshape(UNIT // QUAD, QUAD, 2 * blocks, LANES)
    )


def match_interior(mid_ref, cover_ref, table_ref, shift, weight, out_ref, windows, lines):
    height = mid_ref.shape[0]
    rows = (height - 2 * HALO) // PARTS
    done = 0
    for part in range(PARTS):
        first = HALO + part * rows
        needed = min(-(-(first + rows + HALF + 1) // UNIT), height // UNIT)
        for u in range(done, needed):
            lay_out_unit(mid_ref, u * UNIT, shift, lines[u % len(lines)], windows, u + 1)
        done = needed

        def write(k, e, line, first=first):
            r = first + QUAD * k + e
            good = cover_ref[r].astype(jnp.float32) > 0
            out_ref[r] = (line * jnp.where(good, weight, 0.0)).astype(jnp.bfloat16)

        multiply(windows, [(first // QUAD, rows // QUAD)], table_ref, write)


def late_group():
    return lax.axis_index("tile") % 2 == 1


def first_kernel(
    offset_ref, weight_ref, mask_ref, mid_ref, rows_ref, cols_ref, coeff_ref, cover_ref, out_ref, windows, table_ref, *lines
):
    height, columns = mask_ref.shape
    blocks = columns // LANES
    weight = weight_ref[0]
    for u in range(height // UNIT):
        spot = lines[u % len(lines)]
        rows = slice(u * UNIT, (u + 1) * UNIT)
        good = [mask_ref[rows, lanes_of(h)].astype(jnp.float32) * weight for h in range(blocks)]
        lay_out(good, offset_ref[0], spot, PAD, 4 * blocks)
        tiles = spot[...].reshape(UNIT, 4 * blocks, LANES)
        cover_ref[rows] = tiles[:, PAD : PAD + blocks].astype(jnp.bfloat16)

    @pl.when(late_group())
    def _():
        fill_table(rows_ref, cols_ref, coeff_ref, table_ref)
        shift = offset_ref[0] + HALF
        match_interior(mid_ref, cover_ref, table_ref, shift, weight, out_ref, windows, lines)


def second_kernel(
    offset_ref, weight_ref, low_ref, mid_ref, high_ref, cover_ref, rows_ref, cols_ref, coeff_ref, early_ref, out_ref, windows, table_ref, *lines
):
    height = mid_ref.shape[0]
    weight = weight_ref[0]
    shift = offset_ref[0] + HALF
    late = late_group()
    fill_table(rows_ref, cols_ref, coeff_ref, table_ref)

    @pl.when(late)
    def _():
        out_ref[HALO : height - HALO] = early_ref[HALO : height - HALO]

    @pl.when(jnp.logical_not(late))
    def _():
        match_interior(mid_ref, cover_ref, table_ref, shift, weight, out_ref, windows, lines)

    sources = [
        (low_ref, 0),
        (mid_ref, 0),
        (mid_ref, UNIT),
        (mid_ref, height - 2 * UNIT),
        (mid_ref, height - UNIT),
        (high_ref, 0),
    ]
    for u, (source, first) in enumerate(sources):
        lay_out_unit(source, first, shift, lines[u % len(lines)], windows, u)
    each = HALO // QUAD

    def write(k, e, line):
        r = QUAD * k + e + (0 if k < each else height - 2 * HALO)
        good = cover_ref[r].astype(jnp.float32) > 0
        out_ref[r] = (line * jnp.where(good, weight, 0.0)).astype(jnp.bfloat16)

    multiply(windows, [(0, each), (3 * UNIT // QUAD, each)], table_ref, write)


def window_scratch(height, blocks):
    return pltpu.VMEM((height // QUAD, QUAD, 2 * blocks, LANES), jnp.bfloat16)


def conv_cost(height, columns):
    return pl.CostEstimate(
        flops=2 * height * columns * SHIFTS * LANES, bytes_accessed=8 * 10**6, transcendentals=0
    )


def visit_scratch(height, blocks):
    return [
        window_scratch(height + 2 * HALO, blocks),
        pltpu.VMEM((SHIFTS * LANES, QUAD * SPLIT), jnp.bfloat16),
    ] + [
        pltpu.VMEM((UNIT * 4 * blocks, LANES), jnp.float32)
    ] * 4


def match_first(mid, mask, basis, offset, weight):
    height, columns = mid.shape
    blocks = columns // LANES
    smem = pl.BlockSpec(memory_space=pltpu.SMEM)
    vmem = pl.BlockSpec(memory_space=pltpu.VMEM)
    rows = jax.ShapeDtypeStruct((height, blocks, LANES), jnp.bfloat16)
    return pl.pallas_call(
        first_kernel,
        out_shape=(rows, rows),
        in_specs=[smem, smem] + [vmem] * 5,
        out_specs=(vmem, vmem),
        scratch_shapes=visit_scratch(height, blocks),
        compiler_params=params(),
        cost_estimate=conv_cost(height, columns),
        name="match_first",
    )(offset, weight, mask, mid, *basis)


def match_second(low, mid, high, cover, basis, offset, weight, early):
    height, columns = mid.shape
    blocks = columns // LANES
    smem = pl.BlockSpec(memory_space=pltpu.SMEM)
    vmem = pl.BlockSpec(memory_space=pltpu.VMEM)
    return pl.pallas_call(
        second_kernel,
        out_shape=jax.ShapeDtypeStruct(cover.shape, jnp.bfloat16),
        in_specs=[smem, smem] + [vmem] * 8,
        out_specs=vmem,
        scratch_shapes=visit_scratch(height, blocks),
        compiler_params=params(),
        cost_estimate=conv_cost(height, columns),
        name="match_second",
    )(offset, weight, low, mid, high, cover, *basis, early)


def fill_windows(source, first, padded, windows, unit):
    blocks = source.shape[1]
    turn = SPLIT + HALF
    lane = lax.broadcasted_iota(jnp.int32, (UNIT, blocks, LANES), 2)
    here = source[first : first + UNIT].astype(jnp.float32)
    padded[:, PAD : PAD + blocks] = here
    before = padded[:, PAD - 1 : PAD - 1 + blocks]
    after = padded[:, PAD + 1 : PAD + 1 + blocks]
    left = pltpu.roll(jnp.where(lane < LANES - HALF, here, before), HALF, 2)
    right = pltpu.roll(jnp.where(lane < LANES - turn, after, here), turn, 2)
    both = jnp.concatenate([left, right], axis=1).astype(jnp.bfloat16)
    windows[unit * (UNIT // QUAD) : (unit + 1) * (UNIT // QUAD)] = both.reshape(
        UNIT // QUAD, QUAD, 2 * blocks, LANES
    )


def zero_edges(padded, blocks):
    edge = jnp.zeros((UNIT, PAD, LANES), jnp.float32)
    for spot in padded:
        spot[:, :PAD] = edge
        spot[:, PAD + blocks :] = edge


def interior_kernel(mid_ref, new_ref, table_ref, out_ref, windows, result, lines, sems, *padded):
    height, blocks, _ = mid_ref.shape
    zero_edges(padded, blocks)
    rows = (height - 2 * HALO) // PARTS
    copies = []
    done = 0
    for part in range(PARTS):
        first = HALO + part * rows
        needed = -(-(first + rows + HALF + 1) // UNIT)
        for u in range(done, min(needed, height // UNIT)):
            fill_windows(mid_ref, u * UNIT, padded[u % len(padded)], windows, u + 1)
        done = needed
        spot = lines.at[part % 2]

        def write(k, e, line, spot=spot):
            row = QUAD * k + e
            spot[row * blocks : (row + 1) * blocks, :] = line

        multiply(windows, [(first // QUAD, rows // QUAD)], table_ref, write)
        for h in range(blocks):
            result[first - HALO : first - HALO + rows, lanes_of(h)] = (
                new_ref[first : first + rows, lanes_of(h)].astype(jnp.float32)
                - spot[pl.ds(h, rows, stride=blocks), :]
            )
        copy = pltpu.make_async_copy(
            result.at[pl.ds(first - HALO, rows)], out_ref.at[pl.ds(first, rows)], sems.at[part]
        )
        copy.start()
        copies.append(copy)
    for copy in copies:
        copy.wait()


def subtract_interior(mid, new, table):
    height, blocks, _ = mid.shape
    vmem = pl.BlockSpec(memory_space=pltpu.VMEM)
    rows = (height - 2 * HALO) // PARTS
    return pl.pallas_call(
        interior_kernel,
        out_shape=jax.ShapeDtypeStruct(new.shape, jnp.float32),
        in_specs=[vmem] * 3,
        out_specs=pl.BlockSpec(memory_space=pl.ANY),
        scratch_shapes=[
            window_scratch(height + 2 * HALO, blocks),
            pltpu.VMEM((height - 2 * HALO, blocks * LANES), jnp.float32),
            pltpu.VMEM((2, rows * blocks, LANES), jnp.float32),
            pltpu.SemaphoreType.DMA((PARTS,)),
        ]
        + [pltpu.VMEM((UNIT, blocks + 2 * PAD, LANES), jnp.float32)] * 4,
        compiler_params=params(),
        cost_estimate=conv_cost(*new.shape),
        name="subtract_interior",
    )(mid, new, table)


def edge_kernel(low_ref, mid_ref, high_ref, new_ref, table_ref, _, out_ref, windows, result, lines, sems, *padded):
    height, blocks, _ = mid_ref.shape
    zero_edges(padded, blocks)
    sources = [
        (low_ref, 0),
        (mid_ref, 0),
        (mid_ref, UNIT),
        (mid_ref, height - 2 * UNIT),
        (mid_ref, height - UNIT),
        (high_ref, 0),
    ]
    for u, (source, first) in enumerate(sources):
        fill_windows(source, first, padded[u % len(padded)], windows, u)

    def write(k, e, line):
        row = QUAD * k + e
        lines[row * blocks : (row + 1) * blocks, :] = line

    each = HALO // QUAD
    multiply(windows, [(0, each), (3 * UNIT // QUAD, each)], table_ref, write)
    copies = []
    for side, first in enumerate((0, height - HALO)):
        for h in range(blocks):
            result[side, :, lanes_of(h)] = (
                new_ref[first : first + HALO, lanes_of(h)].astype(jnp.float32)
                - lines[pl.ds(side * HALO * blocks + h, HALO, stride=blocks), :]
            )
        copy = pltpu.make_async_copy(
            result.at[side], out_ref.at[pl.ds(first, HALO)], sems.at[side]
        )
        copy.start()
        copies.append(copy)
    for copy in copies:
        copy.wait()


def subtract_edges(low, mid, high, new, table, difference):
    _, blocks, _ = mid.shape
    vmem = pl.BlockSpec(memory_space=pltpu.VMEM)
    return pl.pallas_call(
        edge_kernel,
        out_shape=jax.ShapeDtypeStruct(difference.shape, difference.dtype),
        in_specs=[vmem] * 5 + [pl.BlockSpec(memory_space=pl.ANY)],
        out_specs=pl.BlockSpec(memory_space=pl.ANY),
        input_output_aliases={5: 0},
        scratch_shapes=[
            window_scratch(6 * UNIT, blocks),
            pltpu.VMEM((2, HALO, blocks * LANES), jnp.float32),
            pltpu.VMEM((2 * HALO * blocks, LANES), jnp.float32),
            pltpu.SemaphoreType.DMA((2,)),
        ]
        + [pltpu.VMEM((UNIT, blocks + 2 * PAD, LANES), jnp.float32)] * 3,
        compiler_params=params(),
        cost_estimate=conv_cost(2 * HALO, new.shape[1]),
        name="subtract_edges",
    )(low, mid, high, new, table, difference)


def add_visits(patch_ref, received_ref, sums):
    sums[...] = jnp.zeros_like(sums)

    def add(v, carry):
        p = patch_ref[v]
        sums[p] = sums[p] + received_ref[v].astype(jnp.float32)
        return carry

    lax.fori_loop(0, received_ref.shape[0], add, 0)


def sum_cover(received, patch_of):
    smem = pl.BlockSpec(memory_space=pltpu.SMEM)
    vmem = pl.BlockSpec(memory_space=pltpu.VMEM)
    return pl.pallas_call(
        add_visits,
        out_shape=jax.ShapeDtypeStruct((PATCHES,) + received.shape[1:], jnp.float32),
        in_specs=[smem, vmem],
        out_specs=vmem,
        compiler_params=params(),
        name="sum_cover",
    )(patch_of, received)


def combine_kernel(
    patch_ref, wanted_ref, received_ref, cover_ref, coadd_ref, send_ref, sums, packed, lines
):
    _, rows, blocks, _ = received_ref.shape
    add_visits(patch_ref, received_ref, sums)
    for p in range(PATCHES):
        ratio = sums[p] / jnp.maximum(cover_ref[p], 1.0)
        packed[p] = ratio.astype(jnp.bfloat16)
        lines[p] = ratio.reshape(rows * blocks, LANES)
        for h in range(blocks):
            coadd_ref[p, :, lanes_of(h)] = lines[p, pl.ds(h, rows, stride=blocks), :].astype(
                jnp.bfloat16
            )

    def place(n, carry):
        send_ref[n] = packed[wanted_ref[n]]
        return carry

    lax.fori_loop(0, send_ref.shape[0], place, 0)


def combine(received, cover_sums, patch_of, new_patch):
    _, rows, blocks, _ = received.shape
    smem = pl.BlockSpec(memory_space=pltpu.SMEM)
    vmem = pl.BlockSpec(memory_space=pltpu.VMEM)
    return pl.pallas_call(
        combine_kernel,
        out_shape=(
            jax.ShapeDtypeStruct((PATCHES, rows, blocks * LANES), jnp.bfloat16),
            jax.ShapeDtypeStruct((new_patch.shape[0], rows, blocks, LANES), jnp.bfloat16),
        ),
        in_specs=[smem, smem, vmem, vmem],
        out_specs=(vmem, vmem),
        scratch_shapes=[
            pltpu.VMEM((PATCHES, rows, blocks, LANES), jnp.float32),
            pltpu.VMEM((PATCHES, rows, blocks, LANES), jnp.bfloat16),
            pltpu.VMEM((PATCHES, rows * blocks, LANES), jnp.float32),
        ],
        compiler_params=params(),
        name="combine",
    )(patch_of, new_patch, received, cover_sums)


def exchange(lines):
    owners = lax.axis_size("visit")
    chunks = lines.reshape((owners, -1) + lines.shape[-2:])
    return lax.all_to_all(chunks, "visit", split_axis=0, concat_axis=0, tiled=True)


def per_device(
    visit_image,
    good_mask,
    basis_rows,
    basis_cols,
    visit_coeff,
    visit_weight,
    col_offset,
    patch_of,
    new_image,
    new_coeff,
    new_patch,
):
    basis = (basis_rows.T, basis_cols.T, visit_coeff)
    cover, early = match_first(
        visit_image[0], good_mask[0], basis, col_offset, visit_weight
    )
    received_cover = exchange(cover)
    low, high = neighbours(visit_image[0], "tile")
    weighted = match_second(
        low, visit_image[0], high, cover, basis, col_offset, visit_weight, early
    )
    received = exchange(weighted)
    cover_sums = sum_cover(received_cover, patch_of[:, 0])
    new_coeff, cover_sums = lax.optimization_barrier((new_coeff, cover_sums))
    new_table = build_table(basis_rows, basis_cols, new_coeff)
    new_table, cover_sums = lax.optimization_barrier((new_table, cover_sums))
    coadd, wanted = combine(received, cover_sums, patch_of[:, 0], new_patch[:, 0])
    template = exchange(wanted)
    template = template.reshape((-1,) + template.shape[2:])
    low, high = neighbours(template, "tile")
    difference = subtract_interior(template, new_image[0], new_table)
    difference = subtract_edges(low, template, high, new_image[0], new_table, difference)
    return (coadd[:, None], difference[None])


def solution(mesh):
    return jax.shard_map(
        per_device,
        mesh=mesh,
        in_specs=(
            P("visit", "tile", None),
            P("visit", "tile", None),
            P(),
            P(),
            P("visit", None),
            P("visit"),
            P("visit"),
            P(),
            P("visit", "tile", None),
            P("visit", None),
            P(),
        ),
        out_specs=(P(None, "tile", "visit", None), P("visit", "tile", None)),
        check_vma=False,
    )
```

```python
import functools

import jax
import jax.numpy as jnp
from jax import lax
from jax.experimental import pallas as pl
from jax.experimental.pallas import tpu as pltpu
from jax.sharding import PartitionSpec as P

KS = 21
HALF = KS // 2
PATCHES = 8
LANES = 128
HALO = 16
QUAD = 4
SPLIT = LANES // 2
SHIFTS = QUAD + KS - 1
CHUNK = 64
PARTS = 4
UNIT = 16
PAD = 8
VMEM_LIMIT = 16 * 2**20


def params():
    return pltpu.CompilerParams(vmem_limit_bytes=VMEM_LIMIT)


def neighbours(block, axis):
    count = lax.axis_size(axis)
    forward = [(i, i + 1) for i in range(count - 1)]
    backward = [(target, source) for source, target in forward]
    low = lax.ppermute(block[-HALO:], axis, forward)
    high = lax.ppermute(block[:HALO], axis, backward)
    return low, high


def fill_table(rows_ref, cols_ref, coeff_ref, table_ref):
    wide = QUAD * SPLIT
    tap = lax.broadcasted_iota(jnp.int32, (KS, wide), 0)
    place = lax.broadcasted_iota(jnp.int32, (KS, wide), 1)
    shift = lax.broadcasted_iota(jnp.int32, (SHIFTS, KS), 0)
    row_tap = lax.broadcasted_iota(jnp.int32, (SHIFTS, KS), 1)
    lane = lax.broadcasted_iota(jnp.int32, (LANES, wide), 0)
    column = lax.broadcasted_iota(jnp.int32, (LANES, wide), 1) % SPLIT
    inside = (lane >= column) & (lane - column < KS)
    kernel = lax.dot_general(
        rows_ref[...] * coeff_ref[...],
        cols_ref[...],
        (((1,), (1,)), ((), ())),
        precision=lax.Precision.HIGHEST,
        preferred_element_type=jnp.float32,
    ).astype(jnp.bfloat16)
    profile = jnp.zeros((SHIFTS, wide), jnp.float32)
    for e in range(QUAD):
        at = (SPLIT * e - tap) % wide
        spread = jnp.dot(
            kernel, (place == at).astype(jnp.bfloat16), preferred_element_type=jnp.float32
        )
        lowered = (shift - e == row_tap).astype(jnp.bfloat16)
        profile = profile + jnp.dot(
            lowered, spread.astype(jnp.bfloat16), preferred_element_type=jnp.float32
        )
    for s in range(SHIFTS):
        line = jnp.broadcast_to(profile[s : s + 1], (LANES, wide))
        rolled = pltpu.roll(line, 0, 1, stride=1, stride_axis=0)
        table_ref[s * LANES : (s + 1) * LANES, :] = jnp.where(inside, rolled, 0.0).astype(
            jnp.bfloat16
        )


def build_table(basis_rows, basis_cols, coeff):
    return pl.pallas_call(
        fill_table,
        out_shape=jax.ShapeDtypeStruct((SHIFTS * LANES, QUAD * SPLIT), jnp.bfloat16),
        compiler_params=params(),
        cost_estimate=pl.CostEstimate(flops=10**9, bytes_accessed=2 * 10**6, transcendentals=0),
        name="table",
    )(basis_rows.T, basis_cols.T, coeff)


def split_shift(shift):
    turn = lax.rem(shift + 2 * LANES, LANES)
    return turn, (turn - shift) // LANES


def lay_out(blocks_of, shift, lines, base, pitch):
    turn, back = split_shift(shift)
    count = blocks_of[0].shape[0]
    lane = lax.broadcasted_iota(jnp.int32, (count, LANES), 1)
    before = jnp.zeros((count, LANES), blocks_of[0].dtype)
    for k in range(len(blocks_of) + 1):
        here = pltpu.roll(blocks_of[k], turn, 1) if k < len(blocks_of) else jnp.zeros_like(before)
        lines[pl.ds(base + k - back, count, stride=pitch), :] = jnp.where(
            lane >= turn, here, before
        )
        before = here


def lanes_of(h):
    return slice(h * LANES, (h + 1) * LANES)


def multiply(windows, starts, table_ref, write):
    parts = []
    for s in range(SHIFTS):
        at = s + HALO - HALF
        pieces = [
            windows[first + at // QUAD : first + at // QUAD + count, at % QUAD]
            for first, count in starts
        ]
        part = pieces[0] if len(pieces) == 1 else jnp.concatenate(pieces, axis=0)
        parts.append(part.reshape(-1, LANES))
    product = jnp.dot(
        jnp.concatenate(parts, axis=1), table_ref[...], preferred_element_type=jnp.float32
    )
    blocks = windows.shape[2] // 2
    lane = lax.broadcasted_iota(jnp.int32, (blocks, LANES), 1)
    for k in range(sum(count for _, count in starts)):
        for pair in range(QUAD // 2):
            a = product[(2 * k) * blocks : (2 * k + 1) * blocks, lanes_of(pair)]
            b = product[(2 * k + 1) * blocks : (2 * k + 2) * blocks, lanes_of(pair)]
            crossed = pltpu.roll(jnp.where(lane < SPLIT, b, a), SPLIT, 1)
            write(k, 2 * pair, jnp.where(lane < SPLIT, a, crossed))
            write(k, 2 * pair + 1, jnp.where(lane < SPLIT, crossed, b))


def lay_out_unit(source, first, shift, spot, windows, unit):
    blocks = windows.shape[2] // 2
    pitch = 4 * blocks
    pixels = [source[first : first + UNIT, lanes_of(h)].astype(jnp.float32) for h in range(blocks)]
    lay_out(pixels, shift, spot, PAD, pitch)
    lay_out(pixels, shift - SPLIT, spot, PAD + 2 * blocks, pitch)
    tiles = spot[...].reshape(UNIT, pitch, LANES)
    both = [tiles[:, PAD + 2 * blocks * k : PAD + 2 * blocks * k + blocks] for k in range(2)]
    windows[unit * (UNIT // QUAD) : (unit + 1) * (UNIT // QUAD)] = (
        jnp.concatenate(both, axis=1)
        .astype(jnp.bfloat16)
        .reshape(UNIT // QUAD, QUAD, 2 * blocks, LANES)
    )


def match_kernel(turn, *refs):
    offset_ref, weight_ref = refs[:2]
    operands = refs[2:9]
    out_ref, windows, table_ref, result, sems, *rest = refs[9 if turn == 0 else 10 :]
    held, lines = rest[:7], rest[7:]

    @pl.when(lax.axis_index("tile") % 2 == 1 - turn)
    def _():
        copies = [
            pltpu.make_async_copy(source, target, sems.at[i])
            for i, (source, target) in enumerate(zip(operands, held))
        ]
        for copy in copies:
            copy.start()
        for copy in copies:
            copy.wait()
        low, mid, high, cover, rows, cols, coeff = held
        fill_table(rows, cols, coeff, table_ref)
        height = mid.shape[0]
        weight = weight_ref[0]
        shift = offset_ref[0] + HALF
        units = height // UNIT + 2
        done = 0
        copies = []
        for first in range(0, height, CHUNK):
            needed = min((first + CHUNK + 2 * HALO) // UNIT, units)
            for u in range(done, needed):
                if u == 0:
                    source, at = low, 0
                elif u == units - 1:
                    source, at = high, 0
                else:
                    source, at = mid, (u - 1) * UNIT
                lay_out_unit(source, at, shift, lines[u % len(lines)], windows, u)
            done = needed

            def write(k, e, line, first=first):
                r = first + QUAD * k + e
                good = cover[r].astype(jnp.float32) > 0
                result[r] = (line * jnp.where(good, weight, 0.0)).astype(jnp.bfloat16)

            multiply(windows, [(first // QUAD, CHUNK // QUAD)], table_ref, write)
            part = pl.ds(first, CHUNK)
            copy = pltpu.make_async_copy(
                result.at[part], out_ref.at[part], sems.at[first // CHUNK]
            )
            copy.start()
            copies.append(copy)
        for copy in copies:
            copy.wait()


def cover_kernel(offset_ref, weight_ref, mask_ref, out_ref, *lines):
    height, columns = mask_ref.shape
    blocks = columns // LANES
    weight = weight_ref[0]
    for u in range(height // UNIT):
        spot = lines[u % len(lines)]
        rows = slice(u * UNIT, (u + 1) * UNIT)
        good = [mask_ref[rows, lanes_of(h)].astype(jnp.float32) * weight for h in range(blocks)]
        lay_out(good, offset_ref[0], spot, PAD, 2 * blocks)
        tiles = spot[...].reshape(UNIT, 2 * blocks, LANES)
        out_ref[rows] = tiles[:, PAD : PAD + blocks].astype(jnp.bfloat16)


def cover_rows(offset, weight, mask):
    height, columns = mask.shape
    blocks = columns // LANES
    smem = pl.BlockSpec(memory_space=pltpu.SMEM)
    vmem = pl.BlockSpec(memory_space=pltpu.VMEM)
    return pl.pallas_call(
        cover_kernel,
        out_shape=jax.ShapeDtypeStruct((height, blocks, LANES), jnp.bfloat16),
        in_specs=[smem, smem, vmem],
        out_specs=vmem,
        scratch_shapes=[pltpu.VMEM((UNIT * 2 * blocks, LANES), jnp.float32)] * 4,
        compiler_params=params(),
        cost_estimate=pl.CostEstimate(flops=10**6, bytes_accessed=6 * 10**6, transcendentals=0),
        name="cover_rows",
    )(offset, weight, mask)


def window_scratch(height, blocks):
    return pltpu.VMEM((height // QUAD, QUAD, 2 * blocks, LANES), jnp.bfloat16)


def conv_cost(height, columns):
    return pl.CostEstimate(
        flops=2 * height * columns * SHIFTS * LANES, bytes_accessed=8 * 10**6, transcendentals=0
    )


def match_visit(turn, offset, weight, operands, *before):
    height, columns = operands[1].shape
    blocks = columns // LANES
    smem = pl.BlockSpec(memory_space=pltpu.SMEM)
    anywhere = pl.BlockSpec(memory_space=pl.ANY)
    rows = (height, blocks, LANES)
    return pl.pallas_call(
        functools.partial(match_kernel, turn),
        out_shape=jax.ShapeDtypeStruct(rows, jnp.bfloat16),
        in_specs=[smem, smem] + [anywhere] * (len(operands) + len(before)),
        out_specs=anywhere,
        input_output_aliases={9: 0} if before else {},
        scratch_shapes=[
            window_scratch(height + 2 * HALO, blocks),
            pltpu.VMEM((SHIFTS * LANES, QUAD * SPLIT), jnp.bfloat16),
            pltpu.VMEM(rows, jnp.bfloat16),
            pltpu.SemaphoreType.DMA((len(operands),)),
        ]
        + [pltpu.VMEM(a.shape, a.dtype) for a in operands]
        + [pltpu.VMEM((UNIT * 4 * blocks, LANES), jnp.float32)] * 4,
        compiler_params=pltpu.CompilerParams(vmem_limit_bytes=56 * 2**20),
        cost_estimate=conv_cost(height, columns),
        name="match_visit",
    )(offset, weight, *operands, *before)


def fill_windows(source, first, padded, windows, unit):
    blocks = source.shape[1]
    turn = SPLIT + HALF
    lane = lax.broadcasted_iota(jnp.int32, (UNIT, blocks, LANES), 2)
    here = source[first : first + UNIT].astype(jnp.float32)
    padded[:, PAD : PAD + blocks] = here
    before = padded[:, PAD - 1 : PAD - 1 + blocks]
    after = padded[:, PAD + 1 : PAD + 1 + blocks]
    left = pltpu.roll(jnp.where(lane < LANES - HALF, here, before), HALF, 2)
    right = pltpu.roll(jnp.where(lane < LANES - turn, after, here), turn, 2)
    both = jnp.concatenate([left, right], axis=1).astype(jnp.bfloat16)
    windows[unit * (UNIT // QUAD) : (unit + 1) * (UNIT // QUAD)] = both.reshape(
        UNIT // QUAD, QUAD, 2 * blocks, LANES
    )


def zero_edges(padded, blocks):
    edge = jnp.zeros((UNIT, PAD, LANES), jnp.float32)
    for spot in padded:
        spot[:, :PAD] = edge
        spot[:, PAD + blocks :] = edge


def interior_kernel(mid_ref, new_ref, table_ref, out_ref, windows, result, lines, sems, *padded):
    height, blocks, _ = mid_ref.shape
    zero_edges(padded, blocks)
    rows = (height - 2 * HALO) // PARTS
    copies = []
    done = 0
    for part in range(PARTS):
        first = HALO + part * rows
        needed = -(-(first + rows + HALF + 1) // UNIT)
        for u in range(done, min(needed, height // UNIT)):
            fill_windows(mid_ref, u * UNIT, padded[u % len(padded)], windows, u + 1)
        done = needed
        spot = lines.at[part % 2]

        def write(k, e, line, spot=spot):
            row = QUAD * k + e
            spot[row * blocks : (row + 1) * blocks, :] = line

        multiply(windows, [(first // QUAD, rows // QUAD)], table_ref, write)
        for h in range(blocks):
            result[first - HALO : first - HALO + rows, lanes_of(h)] = (
                new_ref[first : first + rows, lanes_of(h)].astype(jnp.float32)
                - spot[pl.ds(h, rows, stride=blocks), :]
            )
        copy = pltpu.make_async_copy(
            result.at[pl.ds(first - HALO, rows)], out_ref.at[pl.ds(first, rows)], sems.at[part]
        )
        copy.start()
        copies.append(copy)
    for copy in copies:
        copy.wait()


def subtract_interior(mid, new, table):
    height, blocks, _ = mid.shape
    vmem = pl.BlockSpec(memory_space=pltpu.VMEM)
    rows = (height - 2 * HALO) // PARTS
    return pl.pallas_call(
        interior_kernel,
        out_shape=jax.ShapeDtypeStruct(new.shape, jnp.float32),
        in_specs=[vmem] * 3,
        out_specs=pl.BlockSpec(memory_space=pl.ANY),
        scratch_shapes=[
            window_scratch(height + 2 * HALO, blocks),
            pltpu.VMEM((height - 2 * HALO, blocks * LANES), jnp.float32),
            pltpu.VMEM((2, rows * blocks, LANES), jnp.float32),
            pltpu.SemaphoreType.DMA((PARTS,)),
        ]
        + [pltpu.VMEM((UNIT, blocks + 2 * PAD, LANES), jnp.float32)] * 4,
        compiler_params=params(),
        cost_estimate=conv_cost(*new.shape),
        name="subtract_interior",
    )(mid, new, table)


def edge_kernel(low_ref, mid_ref, high_ref, new_ref, table_ref, _, out_ref, windows, result, lines, sems, *padded):
    height, blocks, _ = mid_ref.shape
    zero_edges(padded, blocks)
    sources = [
        (low_ref, 0),
        (mid_ref, 0),
        (mid_ref, UNIT),
        (mid_ref, height - 2 * UNIT),
        (mid_ref, height - UNIT),
        (high_ref, 0),
    ]
    for u, (source, first) in enumerate(sources):
        fill_windows(source, first, padded[u % len(padded)], windows, u)

    def write(k, e, line):
        row = QUAD * k + e
        lines[row * blocks : (row + 1) * blocks, :] = line

    each = HALO // QUAD
    multiply(windows, [(0, each), (3 * UNIT // QUAD, each)], table_ref, write)
    copies = []
    for side, first in enumerate((0, height - HALO)):
        for h in range(blocks):
            result[side, :, lanes_of(h)] = (
                new_ref[first : first + HALO, lanes_of(h)].astype(jnp.float32)
                - lines[pl.ds(side * HALO * blocks + h, HALO, stride=blocks), :]
            )
        copy = pltpu.make_async_copy(
            result.at[side], out_ref.at[pl.ds(first, HALO)], sems.at[side]
        )
        copy.start()
        copies.append(copy)
    for copy in copies:
        copy.wait()


def subtract_edges(low, mid, high, new, table, difference):
    _, blocks, _ = mid.shape
    vmem = pl.BlockSpec(memory_space=pltpu.VMEM)
    return pl.pallas_call(
        edge_kernel,
        out_shape=jax.ShapeDtypeStruct(difference.shape, difference.dtype),
        in_specs=[vmem] * 5 + [pl.BlockSpec(memory_space=pl.ANY)],
        out_specs=pl.BlockSpec(memory_space=pl.ANY),
        input_output_aliases={5: 0},
        scratch_shapes=[
            window_scratch(6 * UNIT, blocks),
            pltpu.VMEM((2, HALO, blocks * LANES), jnp.float32),
            pltpu.VMEM((2 * HALO * blocks, LANES), jnp.float32),
            pltpu.SemaphoreType.DMA((2,)),
        ]
        + [pltpu.VMEM((UNIT, blocks + 2 * PAD, LANES), jnp.float32)] * 3,
        compiler_params=params(),
        cost_estimate=conv_cost(2 * HALO, new.shape[1]),
        name="subtract_edges",
    )(low, mid, high, new, table, difference)


def add_visits(patch_ref, received_ref, sums):
    sums[...] = jnp.zeros_like(sums)

    def add(v, carry):
        p = patch_ref[v]
        sums[p] = sums[p] + received_ref[v].astype(jnp.float32)
        return carry

    lax.fori_loop(0, received_ref.shape[0], add, 0)


def sum_cover(received, patch_of):
    smem = pl.BlockSpec(memory_space=pltpu.SMEM)
    vmem = pl.BlockSpec(memory_space=pltpu.VMEM)
    return pl.pallas_call(
        add_visits,
        out_shape=jax.ShapeDtypeStruct((PATCHES,) + received.shape[1:], jnp.float32),
        in_specs=[smem, vmem],
        out_specs=vmem,
        compiler_params=params(),
        name="sum_cover",
    )(patch_of, received)


def combine_kernel(
    patch_ref, wanted_ref, received_ref, cover_ref, coadd_ref, send_ref, sums, packed, lines
):
    _, rows, blocks, _ = received_ref.shape
    add_visits(patch_ref, received_ref, sums)
    for p in range(PATCHES):
        ratio = sums[p] / jnp.maximum(cover_ref[p], 1.0)
        packed[p] = ratio.astype(jnp.bfloat16)
        lines[p] = ratio.reshape(rows * blocks, LANES)
        for h in range(blocks):
            coadd_ref[p, :, lanes_of(h)] = lines[p, pl.ds(h, rows, stride=blocks), :].astype(
                jnp.bfloat16
            )

    def place(n, carry):
        send_ref[n] = packed[wanted_ref[n]]
        return carry

    lax.fori_loop(0, send_ref.shape[0], place, 0)


def combine(received, cover_sums, patch_of, new_patch):
    _, rows, blocks, _ = received.shape
    smem = pl.BlockSpec(memory_space=pltpu.SMEM)
    vmem = pl.BlockSpec(memory_space=pltpu.VMEM)
    return pl.pallas_call(
        combine_kernel,
        out_shape=(
            jax.ShapeDtypeStruct((PATCHES, rows, blocks * LANES), jnp.bfloat16),
            jax.ShapeDtypeStruct((new_patch.shape[0], rows, blocks, LANES), jnp.bfloat16),
        ),
        in_specs=[smem, smem, vmem, vmem],
        out_specs=(vmem, vmem),
        scratch_shapes=[
            pltpu.VMEM((PATCHES, rows, blocks, LANES), jnp.float32),
            pltpu.VMEM((PATCHES, rows, blocks, LANES), jnp.bfloat16),
            pltpu.VMEM((PATCHES, rows * blocks, LANES), jnp.float32),
        ],
        compiler_params=params(),
        name="combine",
    )(patch_of, new_patch, received, cover_sums)


def exchange(lines):
    owners = lax.axis_size("visit")
    chunks = lines.reshape((owners, -1) + lines.shape[-2:])
    return lax.all_to_all(chunks, "visit", split_axis=0, concat_axis=0, tiled=True)


def per_device(
    visit_image,
    good_mask,
    basis_rows,
    basis_cols,
    visit_coeff,
    visit_weight,
    col_offset,
    patch_of,
    new_image,
    new_coeff,
    new_patch,
):
    low, high = neighbours(visit_image[0], "tile")
    cover = cover_rows(col_offset, visit_weight, good_mask[0])
    operands = (low, visit_image[0], high, cover, basis_rows.T, basis_cols.T, visit_coeff)
    weighted = match_visit(0, col_offset, visit_weight, operands)
    cover, weighted = lax.optimization_barrier((cover, weighted))
    received_cover = exchange(cover)
    weighted = match_visit(1, col_offset, visit_weight, operands, weighted)
    received = exchange(weighted)
    cover_sums = sum_cover(received_cover, patch_of[:, 0])
    new_coeff, cover_sums = lax.optimization_barrier((new_coeff, cover_sums))
    new_table = build_table(basis_rows, basis_cols, new_coeff)
    new_table, cover_sums = lax.optimization_barrier((new_table, cover_sums))
    coadd, wanted = combine(received, cover_sums, patch_of[:, 0], new_patch[:, 0])
    template = exchange(wanted)
    template = template.reshape((-1,) + template.shape[2:])
    low, high = neighbours(template, "tile")
    difference = subtract_interior(template, new_image[0], new_table)
    difference = subtract_edges(low, template, high, new_image[0], new_table, difference)
    return (coadd[:, None], difference[None])


def solution(mesh):
    return jax.shard_map(
        per_device,
        mesh=mesh,
        in_specs=(
            P("visit", "tile", None),
            P("visit", "tile", None),
            P(),
            P(),
            P("visit", None),
            P("visit"),
            P("visit"),
            P(),
            P("visit", "tile", None),
            P("visit", None),
            P(),
        ),
        out_specs=(P(None, "tile", "visit", None), P("visit", "tile", None)),
        check_vma=False,
    )
```

```python
import functools

import jax
import jax.numpy as jnp
from jax import lax
from jax.experimental import pallas as pl
from jax.experimental.pallas import tpu as pltpu
from jax.sharding import PartitionSpec as P

KS = 21
HALF = KS // 2
PATCHES = 8
LANES = 128
HALO = 16
QUAD = 4
SPLIT = LANES // 2
SHIFTS = QUAD + KS - 1
CHUNK = 64
PARTS = 4
UNIT = 16
PAD = 8
VMEM_LIMIT = 16 * 2**20


def params():
    return pltpu.CompilerParams(vmem_limit_bytes=VMEM_LIMIT)


def roomy():
    return pltpu.CompilerParams(vmem_limit_bytes=56 * 2**20)


def neighbours(block, axis, *after):
    count = lax.axis_size(axis)
    forward = [(i, i + 1) for i in range(count - 1)]
    backward = [(target, source) for source, target in forward]
    top, bottom = block[:HALO], block[-HALO:]
    if after:
        top, bottom, *after = lax.optimization_barrier((top, bottom, *after))
    low = lax.ppermute(bottom, axis, forward)
    high = lax.ppermute(top, axis, backward)
    return low, high, *after


def fill_table(rows_ref, cols_ref, coeff_ref, table_ref):
    wide = QUAD * SPLIT
    tap = lax.broadcasted_iota(jnp.int32, (KS, wide), 0)
    place = lax.broadcasted_iota(jnp.int32, (KS, wide), 1)
    shift = lax.broadcasted_iota(jnp.int32, (SHIFTS, KS), 0)
    row_tap = lax.broadcasted_iota(jnp.int32, (SHIFTS, KS), 1)
    lane = lax.broadcasted_iota(jnp.int32, (LANES, wide), 0)
    column = lax.broadcasted_iota(jnp.int32, (LANES, wide), 1) % SPLIT
    inside = (lane >= column) & (lane - column < KS)
    kernel = lax.dot_general(
        rows_ref[...] * coeff_ref[...],
        cols_ref[...],
        (((1,), (1,)), ((), ())),
        precision=lax.Precision.HIGHEST,
        preferred_element_type=jnp.float32,
    ).astype(jnp.bfloat16)
    profile = jnp.zeros((SHIFTS, wide), jnp.float32)
    for e in range(QUAD):
        at = (SPLIT * e - tap) % wide
        spread = jnp.dot(
            kernel, (place == at).astype(jnp.bfloat16), preferred_element_type=jnp.float32
        )
        lowered = (shift - e == row_tap).astype(jnp.bfloat16)
        profile = profile + jnp.dot(
            lowered, spread.astype(jnp.bfloat16), preferred_element_type=jnp.float32
        )
    for s in range(SHIFTS):
        line = jnp.broadcast_to(profile[s : s + 1], (LANES, wide))
        rolled = pltpu.roll(line, 0, 1, stride=1, stride_axis=0)
        table_ref[s * LANES : (s + 1) * LANES, :] = jnp.where(inside, rolled, 0.0).astype(
            jnp.bfloat16
        )


def build_table(basis_rows, basis_cols, coeff):
    return pl.pallas_call(
        fill_table,
        out_shape=jax.ShapeDtypeStruct((SHIFTS * LANES, QUAD * SPLIT), jnp.bfloat16),
        compiler_params=params(),
        cost_estimate=pl.CostEstimate(flops=10**9, bytes_accessed=2 * 10**6, transcendentals=0),
        name="table",
    )(basis_rows.T, basis_cols.T, coeff)


def split_shift(shift):
    turn = lax.rem(shift + 2 * LANES, LANES)
    return turn, (turn - shift) // LANES


def lay_out(blocks_of, shift, lines, base, pitch):
    turn, back = split_shift(shift)
    count = blocks_of[0].shape[0]
    lane = lax.broadcasted_iota(jnp.int32, (count, LANES), 1)
    before = jnp.zeros((count, LANES), blocks_of[0].dtype)
    for k in range(len(blocks_of) + 1):
        here = pltpu.roll(blocks_of[k], turn, 1) if k < len(blocks_of) else jnp.zeros_like(before)
        lines[pl.ds(base + k - back, count, stride=pitch), :] = jnp.where(
            lane >= turn, here, before
        )
        before = here


def lanes_of(h):
    return slice(h * LANES, (h + 1) * LANES)


def multiply(windows, starts, table_ref, write):
    parts = []
    for s in range(SHIFTS):
        at = s + HALO - HALF
        pieces = [
            windows[first + at // QUAD : first + at // QUAD + count, at % QUAD]
            for first, count in starts
        ]
        part = pieces[0] if len(pieces) == 1 else jnp.concatenate(pieces, axis=0)
        parts.append(part.reshape(-1, LANES))
    product = jnp.dot(
        jnp.concatenate(parts, axis=1), table_ref[...], preferred_element_type=jnp.float32
    )
    blocks = windows.shape[2] // 2
    lane = lax.broadcasted_iota(jnp.int32, (blocks, LANES), 1)
    for k in range(sum(count for _, count in starts)):
        for pair in range(QUAD // 2):
            a = product[(2 * k) * blocks : (2 * k + 1) * blocks, lanes_of(pair)]
            b = product[(2 * k + 1) * blocks : (2 * k + 2) * blocks, lanes_of(pair)]
            crossed = pltpu.roll(jnp.where(lane < SPLIT, b, a), SPLIT, 1)
            write(k, 2 * pair, jnp.where(lane < SPLIT, a, crossed))
            write(k, 2 * pair + 1, jnp.where(lane < SPLIT, crossed, b))


def lay_out_unit(source, first, shift, spot, windows, unit):
    blocks = windows.shape[2] // 2
    pitch = 4 * blocks
    pixels = [source[first : first + UNIT, lanes_of(h)].astype(jnp.float32) for h in range(blocks)]
    lay_out(pixels, shift, spot, PAD, pitch)
    lay_out(pixels, shift - SPLIT, spot, PAD + 2 * blocks, pitch)
    tiles = spot[...].reshape(UNIT, pitch, LANES)
    both = [tiles[:, PAD + 2 * blocks * k : PAD + 2 * blocks * k + blocks] for k in range(2)]
    windows[unit * (UNIT // QUAD) : (unit + 1) * (UNIT // QUAD)] = (
        jnp.concatenate(both, axis=1)
        .astype(jnp.bfloat16)
        .reshape(UNIT // QUAD, QUAD, 2 * blocks, LANES)
    )


def start_copies(pairs, sems):
    copies = [
        pltpu.make_async_copy(source, target, sems.at[i])
        for i, (source, target) in enumerate(pairs)
    ]
    for copy in copies:
        copy.start()
    return copies


def weigh(line, cover, weight):
    good = cover.astype(jnp.float32) > 0
    return (line * jnp.where(good, weight, 0.0)).astype(jnp.bfloat16)


def match_kernel(turn, *refs):
    offset_ref, weight_ref = refs[:2]
    operands = refs[2:7]
    out_ref, windows, table_ref, result, sems, *rest = refs[7 if turn == 0 else 8 :]
    held, lines = rest[:5], rest[5:]

    @pl.when(lax.axis_index("tile") % 2 == 1 - turn)
    def _():
        for copy in start_copies(zip(operands, held), sems):
            copy.wait()
        mid, cover, rows, cols, coeff = held
        fill_table(rows, cols, coeff, table_ref)
        height = mid.shape[0]
        weight = weight_ref[0]
        shift = offset_ref[0] + HALF
        each = (height - 2 * HALO) // PARTS
        done = 0
        copies = []
        for part in range(PARTS):
            first = HALO + part * each
            needed = min(-(-(first + each + HALF + 1) // UNIT), height // UNIT)
            for u in range(done, needed):
                lay_out_unit(mid, u * UNIT, shift, lines[u % len(lines)], windows, u + 1)
            done = needed

            def write(k, e, line, first=first):
                r = first + QUAD * k + e
                result[r] = weigh(line, cover[r], weight)

            multiply(windows, [(first // QUAD, each // QUAD)], table_ref, write)
            span = pl.ds(first, each)
            copy = pltpu.make_async_copy(result.at[span], out_ref.at[span], sems.at[part])
            copy.start()
            copies.append(copy)
        for copy in copies:
            copy.wait()


def match_edge_kernel(
    offset_ref, weight_ref, low, mid, high, cover, rows, cols, coeff, _, out_ref, windows, table_ref, result, sems, *lines
):
    height = mid.shape[0]
    weight = weight_ref[0]
    shift = offset_ref[0] + HALF
    fill_table(rows, cols, coeff, table_ref)
    sources = [
        (low, 0),
        (mid, 0),
        (mid, UNIT),
        (mid, height - 2 * UNIT),
        (mid, height - UNIT),
        (high, 0),
    ]
    for u, (source, first) in enumerate(sources):
        lay_out_unit(source, first, shift, lines[u % len(lines)], windows, u)
    each = HALO // QUAD

    def write(k, e, line):
        side, row = k // each, QUAD * (k % each) + e
        result[side, row] = weigh(line, cover[row + side * (height - HALO)], weight)

    multiply(windows, [(0, each), (3 * UNIT // QUAD, each)], table_ref, write)
    ends = [
        (result.at[side], out_ref.at[pl.ds(first, HALO)])
        for side, first in enumerate((0, height - HALO))
    ]
    for copy in start_copies(ends, sems):
        copy.wait()


def cover_kernel(offset_ref, weight_ref, mask_ref, out_ref, held, sems, *lines):
    height, columns = mask_ref.shape
    blocks = columns // LANES
    weight = weight_ref[0]
    spans = [pl.ds(first, CHUNK) for first in range(0, height, CHUNK)]
    copies = start_copies([(mask_ref.at[s], held.at[s]) for s in spans], sems)
    for u in range(height // UNIT):
        if u % (CHUNK // UNIT) == 0:
            copies[u // (CHUNK // UNIT)].wait()
        spot = lines[u % len(lines)]
        rows = slice(u * UNIT, (u + 1) * UNIT)
        good = [held[rows, lanes_of(h)].astype(jnp.float32) * weight for h in range(blocks)]
        lay_out(good, offset_ref[0], spot, PAD, 2 * blocks)
        tiles = spot[...].reshape(UNIT, 2 * blocks, LANES)
        out_ref[rows] = tiles[:, PAD : PAD + blocks].astype(jnp.bfloat16)


def cover_rows(offset, weight, mask):
    height, columns = mask.shape
    blocks = columns // LANES
    smem = pl.BlockSpec(memory_space=pltpu.SMEM)
    vmem = pl.BlockSpec(memory_space=pltpu.VMEM)
    return pl.pallas_call(
        cover_kernel,
        out_shape=jax.ShapeDtypeStruct((height, blocks, LANES), jnp.bfloat16),
        in_specs=[smem, smem, pl.BlockSpec(memory_space=pl.ANY)],
        out_specs=vmem,
        scratch_shapes=[
            pltpu.VMEM(mask.shape, mask.dtype),
            pltpu.SemaphoreType.DMA((height // CHUNK,)),
        ]
        + [pltpu.VMEM((UNIT * 2 * blocks, LANES), jnp.float32)] * 4,
        compiler_params=roomy(),
        cost_estimate=pl.CostEstimate(flops=10**6, bytes_accessed=6 * 10**6, transcendentals=0),
        name="cover_rows",
    )(offset, weight, mask)


def window_scratch(height, blocks):
    return pltpu.VMEM((height // QUAD, QUAD, 2 * blocks, LANES), jnp.bfloat16)


def conv_cost(height, columns):
    return pl.CostEstimate(
        flops=2 * height * columns * SHIFTS * LANES, bytes_accessed=8 * 10**6, transcendentals=0
    )


def match_visit(turn, offset, weight, operands, *before):
    height, columns = operands[0].shape
    blocks = columns // LANES
    smem = pl.BlockSpec(memory_space=pltpu.SMEM)
    anywhere = pl.BlockSpec(memory_space=pl.ANY)
    rows = (height, blocks, LANES)
    return pl.pallas_call(
        functools.partial(match_kernel, turn),
        out_shape=jax.ShapeDtypeStruct(rows, jnp.bfloat16),
        in_specs=[smem, smem] + [anywhere] * (len(operands) + len(before)),
        out_specs=anywhere,
        input_output_aliases={7: 0} if before else {},
        scratch_shapes=[
            window_scratch(height + 2 * HALO, blocks),
            pltpu.VMEM((SHIFTS * LANES, QUAD * SPLIT), jnp.bfloat16),
            pltpu.VMEM(rows, jnp.bfloat16),
            pltpu.SemaphoreType.DMA((len(operands),)),
        ]
        + [pltpu.VMEM(a.shape, a.dtype) for a in operands]
        + [pltpu.VMEM((UNIT * 4 * blocks, LANES), jnp.float32)] * 4,
        compiler_params=roomy(),
        cost_estimate=conv_cost(height, columns),
        name="match_visit",
    )(offset, weight, *operands, *before)


def match_edges(low, mid, high, cover, basis, offset, weight, weighted):
    _, columns = mid.shape
    blocks = columns // LANES
    smem = pl.BlockSpec(memory_space=pltpu.SMEM)
    vmem = pl.BlockSpec(memory_space=pltpu.VMEM)
    anywhere = pl.BlockSpec(memory_space=pl.ANY)
    return pl.pallas_call(
        match_edge_kernel,
        out_shape=jax.ShapeDtypeStruct(weighted.shape, weighted.dtype),
        in_specs=[smem, smem] + [vmem] * 7 + [anywhere],
        out_specs=anywhere,
        input_output_aliases={9: 0},
        scratch_shapes=[
            window_scratch(6 * UNIT, blocks),
            pltpu.VMEM((SHIFTS * LANES, QUAD * SPLIT), jnp.bfloat16),
            pltpu.VMEM((2, HALO, blocks, LANES), jnp.bfloat16),
            pltpu.SemaphoreType.DMA((2,)),
        ]
        + [pltpu.VMEM((UNIT * 4 * blocks, LANES), jnp.float32)] * 3,
        compiler_params=roomy(),
        cost_estimate=conv_cost(2 * HALO, columns),
        name="match_edges",
    )(offset, weight, low, mid, high, cover, *basis, weighted)


def fill_windows(source, first, padded, windows, unit):
    blocks = source.shape[1]
    turn = SPLIT + HALF
    lane = lax.broadcasted_iota(jnp.int32, (UNIT, blocks, LANES), 2)
    here = source[first : first + UNIT].astype(jnp.float32)
    padded[:, PAD : PAD + blocks] = here
    before = padded[:, PAD - 1 : PAD - 1 + blocks]
    after = padded[:, PAD + 1 : PAD + 1 + blocks]
    left = pltpu.roll(jnp.where(lane < LANES - HALF, here, before), HALF, 2)
    right = pltpu.roll(jnp.where(lane < LANES - turn, after, here), turn, 2)
    both = jnp.concatenate([left, right], axis=1).astype(jnp.bfloat16)
    windows[unit * (UNIT // QUAD) : (unit + 1) * (UNIT // QUAD)] = both.reshape(
        UNIT // QUAD, QUAD, 2 * blocks, LANES
    )


def zero_edges(padded, blocks):
    edge = jnp.zeros((UNIT, PAD, LANES), jnp.float32)
    for spot in padded:
        spot[:, :PAD] = edge
        spot[:, PAD + blocks :] = edge


def interior_kernel(mid_ref, new_ref, table_ref, out_ref, windows, result, lines, sems, *padded):
    height, blocks, _ = mid_ref.shape
    zero_edges(padded, blocks)
    rows = (height - 2 * HALO) // PARTS
    copies = []
    done = 0
    for part in range(PARTS):
        first = HALO + part * rows
        needed = -(-(first + rows + HALF + 1) // UNIT)
        for u in range(done, min(needed, height // UNIT)):
            fill_windows(mid_ref, u * UNIT, padded[u % len(padded)], windows, u + 1)
        done = needed
        spot = lines.at[part % 2]

        def write(k, e, line, spot=spot):
            row = QUAD * k + e
            spot[row * blocks : (row + 1) * blocks, :] = line

        multiply(windows, [(first // QUAD, rows // QUAD)], table_ref, write)
        for h in range(blocks):
            result[first - HALO : first - HALO + rows, lanes_of(h)] = (
                new_ref[first : first + rows, lanes_of(h)].astype(jnp.float32)
                - spot[pl.ds(h, rows, stride=blocks), :]
            )
        copy = pltpu.make_async_copy(
            result.at[pl.ds(first - HALO, rows)], out_ref.at[pl.ds(first, rows)], sems.at[part]
        )
        copy.start()
        copies.append(copy)
    for copy in copies:
        copy.wait()


def subtract_interior(mid, new, table):
    height, blocks, _ = mid.shape
    vmem = pl.BlockSpec(memory_space=pltpu.VMEM)
    rows = (height - 2 * HALO) // PARTS
    return pl.pallas_call(
        interior_kernel,
        out_shape=jax.ShapeDtypeStruct(new.shape, jnp.float32),
        in_specs=[vmem] * 3,
        out_specs=pl.BlockSpec(memory_space=pl.ANY),
        scratch_shapes=[
            window_scratch(height + 2 * HALO, blocks),
            pltpu.VMEM((height - 2 * HALO, blocks * LANES), jnp.float32),
            pltpu.VMEM((2, rows * blocks, LANES), jnp.float32),
            pltpu.SemaphoreType.DMA((PARTS,)),
        ]
        + [pltpu.VMEM((UNIT, blocks + 2 * PAD, LANES), jnp.float32)] * 4,
        compiler_params=params(),
        cost_estimate=conv_cost(*new.shape),
        name="subtract_interior",
    )(mid, new, table)


def edge_kernel(low_ref, mid_ref, high_ref, new_ref, table_ref, _, out_ref, windows, result, lines, sems, *padded):
    height, blocks, _ = mid_ref.shape
    zero_edges(padded, blocks)
    sources = [
        (low_ref, 0),
        (mid_ref, 0),
        (mid_ref, UNIT),
        (mid_ref, height - 2 * UNIT),
        (mid_ref, height - UNIT),
        (high_ref, 0),
    ]
    for u, (source, first) in enumerate(sources):
        fill_windows(source, first, padded[u % len(padded)], windows, u)

    def write(k, e, line):
        row = QUAD * k + e
        lines[row * blocks : (row + 1) * blocks, :] = line

    each = HALO // QUAD
    multiply(windows, [(0, each), (3 * UNIT // QUAD, each)], table_ref, write)
    copies = []
    for side, first in enumerate((0, height - HALO)):
        for h in range(blocks):
            result[side, :, lanes_of(h)] = (
                new_ref[first : first + HALO, lanes_of(h)].astype(jnp.float32)
                - lines[pl.ds(side * HALO * blocks + h, HALO, stride=blocks), :]
            )
        copy = pltpu.make_async_copy(
            result.at[side], out_ref.at[pl.ds(first, HALO)], sems.at[side]
        )
        copy.start()
        copies.append(copy)
    for copy in copies:
        copy.wait()


def subtract_edges(low, mid, high, new, table, difference):
    _, blocks, _ = mid.shape
    vmem = pl.BlockSpec(memory_space=pltpu.VMEM)
    return pl.pallas_call(
        edge_kernel,
        out_shape=jax.ShapeDtypeStruct(difference.shape, difference.dtype),
        in_specs=[vmem] * 5 + [pl.BlockSpec(memory_space=pl.ANY)],
        out_specs=pl.BlockSpec(memory_space=pl.ANY),
        input_output_aliases={5: 0},
        scratch_shapes=[
            window_scratch(6 * UNIT, blocks),
            pltpu.VMEM((2, HALO, blocks * LANES), jnp.float32),
            pltpu.VMEM((2 * HALO * blocks, LANES), jnp.float32),
            pltpu.SemaphoreType.DMA((2,)),
        ]
        + [pltpu.VMEM((UNIT, blocks + 2 * PAD, LANES), jnp.float32)] * 3,
        compiler_params=params(),
        cost_estimate=conv_cost(2 * HALO, new.shape[1]),
        name="subtract_edges",
    )(low, mid, high, new, table, difference)


def add_visits(patch_ref, received_ref, sums):
    sums[...] = jnp.zeros_like(sums)

    def add(v, carry):
        p = patch_ref[v]
        sums[p] = sums[p] + received_ref[v].astype(jnp.float32)
        return carry

    lax.fori_loop(0, received_ref.shape[0], add, 0)


def sum_cover(received, patch_of):
    smem = pl.BlockSpec(memory_space=pltpu.SMEM)
    vmem = pl.BlockSpec(memory_space=pltpu.VMEM)
    return pl.pallas_call(
        add_visits,
        out_shape=jax.ShapeDtypeStruct((PATCHES,) + received.shape[1:], jnp.float32),
        in_specs=[smem, vmem],
        out_specs=vmem,
        compiler_params=params(),
        name="sum_cover",
    )(patch_of, received)


def combine_kernel(
    patch_ref, wanted_ref, received_ref, cover_ref, coadd_ref, send_ref, sums, packed, lines
):
    _, rows, blocks, _ = received_ref.shape
    add_visits(patch_ref, received_ref, sums)
    for p in range(PATCHES):
        ratio = sums[p] / jnp.maximum(cover_ref[p], 1.0)
        packed[p] = ratio.astype(jnp.bfloat16)
        lines[p] = ratio.reshape(rows * blocks, LANES)
        for h in range(blocks):
            coadd_ref[p, :, lanes_of(h)] = lines[p, pl.ds(h, rows, stride=blocks), :].astype(
                jnp.bfloat16
            )

    def place(n, carry):
        send_ref[n] = packed[wanted_ref[n]]
        return carry

    lax.fori_loop(0, send_ref.shape[0], place, 0)


def combine(received, cover_sums, patch_of, new_patch):
    _, rows, blocks, _ = received.shape
    smem = pl.BlockSpec(memory_space=pltpu.SMEM)
    vmem = pl.BlockSpec(memory_space=pltpu.VMEM)
    return pl.pallas_call(
        combine_kernel,
        out_shape=(
            jax.ShapeDtypeStruct((PATCHES, rows, blocks * LANES), jnp.bfloat16),
            jax.ShapeDtypeStruct((new_patch.shape[0], rows, blocks, LANES), jnp.bfloat16),
        ),
        in_specs=[smem, smem, vmem, vmem],
        out_specs=(vmem, vmem),
        scratch_shapes=[
            pltpu.VMEM((PATCHES, rows, blocks, LANES), jnp.float32),
            pltpu.VMEM((PATCHES, rows, blocks, LANES), jnp.bfloat16),
            pltpu.VMEM((PATCHES, rows * blocks, LANES), jnp.float32),
        ],
        compiler_params=params(),
        name="combine",
    )(patch_of, new_patch, received, cover_sums)


def exchange(lines):
    owners = lax.axis_size("visit")
    chunks = lines.reshape((owners, -1) + lines.shape[-2:])
    return lax.all_to_all(chunks, "visit", split_axis=0, concat_axis=0, tiled=True)


def per_device(
    visit_image,
    good_mask,
    basis_rows,
    basis_cols,
    visit_coeff,
    visit_weight,
    col_offset,
    patch_of,
    new_image,
    new_coeff,
    new_patch,
):
    cover = cover_rows(col_offset, visit_weight, good_mask[0])
    basis = (basis_rows.T, basis_cols.T, visit_coeff)
    operands = (visit_image[0], cover, *basis)
    weighted = match_visit(0, col_offset, visit_weight, operands)
    cover, weighted = lax.optimization_barrier((cover, weighted))
    received_cover = exchange(cover)
    weighted = match_visit(1, col_offset, visit_weight, operands, weighted)
    low, high, weighted = neighbours(visit_image[0], "tile", weighted)
    weighted = match_edges(
        low, visit_image[0], high, cover, basis, col_offset, visit_weight, weighted
    )
    received = exchange(weighted)
    cover_sums = sum_cover(received_cover, patch_of[:, 0])
    new_coeff, cover_sums = lax.optimization_barrier((new_coeff, cover_sums))
    new_table = build_table(basis_rows, basis_cols, new_coeff)
    new_table, cover_sums = lax.optimization_barrier((new_table, cover_sums))
    coadd, wanted = combine(received, cover_sums, patch_of[:, 0], new_patch[:, 0])
    template = exchange(wanted)
    template = template.reshape((-1,) + template.shape[2:])
    low, high = neighbours(template, "tile")
    difference = subtract_interior(template, new_image[0], new_table)
    difference = subtract_edges(low, template, high, new_image[0], new_table, difference)
    return (coadd[:, None], difference[None])


def solution(mesh):
    return jax.shard_map(
        per_device,
        mesh=mesh,
        in_specs=(
            P("visit", "tile", None),
            P("visit", "tile", None),
            P(),
            P(),
            P("visit", None),
            P("visit"),
            P("visit"),
            P(),
            P("visit", "tile", None),
            P("visit", None),
            P(),
        ),
        out_specs=(P(None, "tile", "visit", None), P("visit", "tile", None)),
        check_vma=False,
    )
```

```python
import functools

import jax
import jax.numpy as jnp
from jax import lax
from jax.experimental import pallas as pl
from jax.experimental.pallas import tpu as pltpu
from jax.sharding import PartitionSpec as P

KS = 21
HALF = KS // 2
PATCHES = 8
LANES = 128
HALO = 16
QUAD = 4
SPLIT = LANES // 2
SHIFTS = QUAD + KS - 1
CHUNK = 64
PARTS = 4
UNIT = 16
PAD = 8
VMEM_LIMIT = 16 * 2**20


def params():
    return pltpu.CompilerParams(vmem_limit_bytes=VMEM_LIMIT)


def roomy():
    return pltpu.CompilerParams(vmem_limit_bytes=56 * 2**20)


def neighbours(block, axis):
    count = lax.axis_size(axis)
    forward = [(i, i + 1) for i in range(count - 1)]
    backward = [(target, source) for source, target in forward]
    low = lax.ppermute(block[-HALO:], axis, forward)
    high = lax.ppermute(block[:HALO], axis, backward)
    return low, high


def fill_table(rows_ref, cols_ref, coeff_ref, table_ref):
    wide = QUAD * SPLIT
    tap = lax.broadcasted_iota(jnp.int32, (KS, wide), 0)
    place = lax.broadcasted_iota(jnp.int32, (KS, wide), 1)
    shift = lax.broadcasted_iota(jnp.int32, (SHIFTS, KS), 0)
    row_tap = lax.broadcasted_iota(jnp.int32, (SHIFTS, KS), 1)
    lane = lax.broadcasted_iota(jnp.int32, (LANES, wide), 0)
    column = lax.broadcasted_iota(jnp.int32, (LANES, wide), 1) % SPLIT
    inside = (lane >= column) & (lane - column < KS)
    kernel = lax.dot_general(
        rows_ref[...] * coeff_ref[...],
        cols_ref[...],
        (((1,), (1,)), ((), ())),
        precision=lax.Precision.HIGHEST,
        preferred_element_type=jnp.float32,
    ).astype(jnp.bfloat16)
    profile = jnp.zeros((SHIFTS, wide), jnp.float32)
    for e in range(QUAD):
        at = (SPLIT * e - tap) % wide
        spread = jnp.dot(
            kernel, (place == at).astype(jnp.bfloat16), preferred_element_type=jnp.float32
        )
        lowered = (shift - e == row_tap).astype(jnp.bfloat16)
        profile = profile + jnp.dot(
            lowered, spread.astype(jnp.bfloat16), preferred_element_type=jnp.float32
        )
    for s in range(SHIFTS):
        line = jnp.broadcast_to(profile[s : s + 1], (LANES, wide))
        rolled = pltpu.roll(line, 0, 1, stride=1, stride_axis=0)
        table_ref[s * LANES : (s + 1) * LANES, :] = jnp.where(inside, rolled, 0.0).astype(
            jnp.bfloat16
        )


def build_table(basis_rows, basis_cols, coeff):
    return pl.pallas_call(
        fill_table,
        out_shape=jax.ShapeDtypeStruct((SHIFTS * LANES, QUAD * SPLIT), jnp.bfloat16),
        compiler_params=params(),
        cost_estimate=pl.CostEstimate(flops=10**9, bytes_accessed=2 * 10**6, transcendentals=0),
        name="table",
    )(basis_rows.T, basis_cols.T, coeff)


def split_shift(shift):
    turn = lax.rem(shift + 2 * LANES, LANES)
    return turn, (turn - shift) // LANES


def lay_out(blocks_of, shift, lines, base, pitch):
    turn, back = split_shift(shift)
    count = blocks_of[0].shape[0]
    lane = lax.broadcasted_iota(jnp.int32, (count, LANES), 1)
    before = jnp.zeros((count, LANES), blocks_of[0].dtype)
    for k in range(len(blocks_of) + 1):
        here = pltpu.roll(blocks_of[k], turn, 1) if k < len(blocks_of) else jnp.zeros_like(before)
        lines[pl.ds(base + k - back, count, stride=pitch), :] = jnp.where(
            lane >= turn, here, before
        )
        before = here


def lanes_of(h):
    return slice(h * LANES, (h + 1) * LANES)


def multiply(windows, starts, table_ref, write):
    parts = []
    for s in range(SHIFTS):
        at = s + HALO - HALF
        pieces = [
            windows[first + at // QUAD : first + at // QUAD + count, at % QUAD]
            for first, count in starts
        ]
        part = pieces[0] if len(pieces) == 1 else jnp.concatenate(pieces, axis=0)
        parts.append(part.reshape(-1, LANES))
    product = jnp.dot(
        jnp.concatenate(parts, axis=1), table_ref[...], preferred_element_type=jnp.float32
    )
    blocks = windows.shape[2] // 2
    lane = lax.broadcasted_iota(jnp.int32, (blocks, LANES), 1)
    for k in range(sum(count for _, count in starts)):
        for pair in range(QUAD // 2):
            a = product[(2 * k) * blocks : (2 * k + 1) * blocks, lanes_of(pair)]
            b = product[(2 * k + 1) * blocks : (2 * k + 2) * blocks, lanes_of(pair)]
            crossed = pltpu.roll(jnp.where(lane < SPLIT, b, a), SPLIT, 1)
            write(k, 2 * pair, jnp.where(lane < SPLIT, a, crossed))
            write(k, 2 * pair + 1, jnp.where(lane < SPLIT, crossed, b))


def lay_out_unit(source, first, shift, spot, windows, unit):
    blocks = windows.shape[2] // 2
    pitch = 4 * blocks
    pixels = [source[first : first + UNIT, lanes_of(h)].astype(jnp.float32) for h in range(blocks)]
    lay_out(pixels, shift, spot, PAD, pitch)
    lay_out(pixels, shift - SPLIT, spot, PAD + 2 * blocks, pitch)
    tiles = spot[...].reshape(UNIT, pitch, LANES)
    both = [tiles[:, PAD + 2 * blocks * k : PAD + 2 * blocks * k + blocks] for k in range(2)]
    windows[unit * (UNIT // QUAD) : (unit + 1) * (UNIT // QUAD)] = (
        jnp.concatenate(both, axis=1)
        .astype(jnp.bfloat16)
        .reshape(UNIT // QUAD, QUAD, 2 * blocks, LANES)
    )


def match_kernel(turn, *refs):
    offset_ref, weight_ref = refs[:2]
    operands = refs[2:9]
    out_ref, windows, table_ref, result, sems, *rest = refs[9 if turn == 0 else 10 :]
    held, lines = rest[:7], rest[7:]

    @pl.when(lax.axis_index("tile") % 2 == 1 - turn)
    def _():
        copies = [
            pltpu.make_async_copy(source, target, sems.at[i])
            for i, (source, target) in enumerate(zip(operands, held))
        ]
        for copy in copies:
            copy.start()
        for copy in copies:
            copy.wait()
        low, mid, high, cover, rows, cols, coeff = held
        fill_table(rows, cols, coeff, table_ref)
        height = mid.shape[0]
        weight = weight_ref[0]
        shift = offset_ref[0] + HALF
        units = height // UNIT + 2
        done = 0
        copies = []
        for first in range(0, height, CHUNK):
            needed = min((first + CHUNK + 2 * HALO) // UNIT, units)
            for u in range(done, needed):
                if u == 0:
                    source, at = low, 0
                elif u == units - 1:
                    source, at = high, 0
                else:
                    source, at = mid, (u - 1) * UNIT
                lay_out_unit(source, at, shift, lines[u % len(lines)], windows, u)
            done = needed

            def write(k, e, line, first=first):
                r = first + QUAD * k + e
                good = cover[r].astype(jnp.float32) > 0
                result[r] = (line * jnp.where(good, weight, 0.0)).astype(jnp.bfloat16)

            multiply(windows, [(first // QUAD, CHUNK // QUAD)], table_ref, write)
            part = pl.ds(first, CHUNK)
            copy = pltpu.make_async_copy(
                result.at[part], out_ref.at[part], sems.at[first // CHUNK]
            )
            copy.start()
            copies.append(copy)
        for copy in copies:
            copy.wait()


def start_copies(pairs, sems):
    copies = [
        pltpu.make_async_copy(source, target, sems.at[i])
        for i, (source, target) in enumerate(pairs)
    ]
    for copy in copies:
        copy.start()
    return copies


def cover_kernel(offset_ref, weight_ref, mask_ref, out_ref, held, sems, *lines):
    height, columns = mask_ref.shape
    blocks = columns // LANES
    weight = weight_ref[0]
    spans = [pl.ds(first, CHUNK) for first in range(0, height, CHUNK)]
    copies = start_copies([(mask_ref.at[s], held.at[s]) for s in spans], sems)
    for u in range(height // UNIT):
        if u % (CHUNK // UNIT) == 0:
            copies[u // (CHUNK // UNIT)].wait()
        spot = lines[u % len(lines)]
        rows = slice(u * UNIT, (u + 1) * UNIT)
        good = [held[rows, lanes_of(h)].astype(jnp.float32) * weight for h in range(blocks)]
        lay_out(good, offset_ref[0], spot, PAD, 2 * blocks)
        tiles = spot[...].reshape(UNIT, 2 * blocks, LANES)
        out_ref[rows] = tiles[:, PAD : PAD + blocks].astype(jnp.bfloat16)


def cover_rows(offset, weight, mask):
    height, columns = mask.shape
    blocks = columns // LANES
    smem = pl.BlockSpec(memory_space=pltpu.SMEM)
    vmem = pl.BlockSpec(memory_space=pltpu.VMEM)
    return pl.pallas_call(
        cover_kernel,
        out_shape=jax.ShapeDtypeStruct((height, blocks, LANES), jnp.bfloat16),
        in_specs=[smem, smem, pl.BlockSpec(memory_space=pl.ANY)],
        out_specs=vmem,
        scratch_shapes=[
            pltpu.VMEM(mask.shape, mask.dtype),
            pltpu.SemaphoreType.DMA((height // CHUNK,)),
        ]
        + [pltpu.VMEM((UNIT * 2 * blocks, LANES), jnp.float32)] * 4,
        compiler_params=roomy(),
        cost_estimate=pl.CostEstimate(flops=10**6, bytes_accessed=6 * 10**6, transcendentals=0),
        name="cover_rows",
    )(offset, weight, mask)


def window_scratch(height, blocks):
    return pltpu.VMEM((height // QUAD, QUAD, 2 * blocks, LANES), jnp.bfloat16)


def conv_cost(height, columns):
    return pl.CostEstimate(
        flops=2 * height * columns * SHIFTS * LANES, bytes_accessed=8 * 10**6, transcendentals=0
    )


def match_visit(turn, offset, weight, operands, *before):
    height, columns = operands[1].shape
    blocks = columns // LANES
    smem = pl.BlockSpec(memory_space=pltpu.SMEM)
    anywhere = pl.BlockSpec(memory_space=pl.ANY)
    rows = (height, blocks, LANES)
    return pl.pallas_call(
        functools.partial(match_kernel, turn),
        out_shape=jax.ShapeDtypeStruct(rows, jnp.bfloat16),
        in_specs=[smem, smem] + [anywhere] * (len(operands) + len(before)),
        out_specs=anywhere,
        input_output_aliases={9: 0} if before else {},
        scratch_shapes=[
            window_scratch(height + 2 * HALO, blocks),
            pltpu.VMEM((SHIFTS * LANES, QUAD * SPLIT), jnp.bfloat16),
            pltpu.VMEM(rows, jnp.bfloat16),
            pltpu.SemaphoreType.DMA((len(operands),)),
        ]
        + [pltpu.VMEM(a.shape, a.dtype) for a in operands]
        + [pltpu.VMEM((UNIT * 4 * blocks, LANES), jnp.float32)] * 4,
        compiler_params=pltpu.CompilerParams(vmem_limit_bytes=56 * 2**20),
        cost_estimate=conv_cost(height, columns),
        name="match_visit",
    )(offset, weight, *operands, *before)


def fill_windows(source, first, padded, windows, unit):
    blocks = source.shape[1]
    turn = SPLIT + HALF
    lane = lax.broadcasted_iota(jnp.int32, (UNIT, blocks, LANES), 2)
    here = source[first : first + UNIT].astype(jnp.float32)
    padded[:, PAD : PAD + blocks] = here
    before = padded[:, PAD - 1 : PAD - 1 + blocks]
    after = padded[:, PAD + 1 : PAD + 1 + blocks]
    left = pltpu.roll(jnp.where(lane < LANES - HALF, here, before), HALF, 2)
    right = pltpu.roll(jnp.where(lane < LANES - turn, after, here), turn, 2)
    both = jnp.concatenate([left, right], axis=1).astype(jnp.bfloat16)
    windows[unit * (UNIT // QUAD) : (unit + 1) * (UNIT // QUAD)] = both.reshape(
        UNIT // QUAD, QUAD, 2 * blocks, LANES
    )


def zero_edges(padded, blocks):
    edge = jnp.zeros((UNIT, PAD, LANES), jnp.float32)
    for spot in padded:
        spot[:, :PAD] = edge
        spot[:, PAD + blocks :] = edge


def interior_kernel(mid_ref, new_ref, table_ref, out_ref, windows, result, lines, sems, *padded):
    height, blocks, _ = mid_ref.shape
    zero_edges(padded, blocks)
    rows = (height - 2 * HALO) // PARTS
    copies = []
    done = 0
    for part in range(PARTS):
        first = HALO + part * rows
        needed = -(-(first + rows + HALF + 1) // UNIT)
        for u in range(done, min(needed, height // UNIT)):
            fill_windows(mid_ref, u * UNIT, padded[u % len(padded)], windows, u + 1)
        done = needed
        spot = lines.at[part % 2]

        def write(k, e, line, spot=spot):
            row = QUAD * k + e
            spot[row * blocks : (row + 1) * blocks, :] = line

        multiply(windows, [(first // QUAD, rows // QUAD)], table_ref, write)
        for h in range(blocks):
            result[first - HALO : first - HALO + rows, lanes_of(h)] = (
                new_ref[first : first + rows, lanes_of(h)].astype(jnp.float32)
                - spot[pl.ds(h, rows, stride=blocks), :]
            )
        copy = pltpu.make_async_copy(
            result.at[pl.ds(first - HALO, rows)], out_ref.at[pl.ds(first, rows)], sems.at[part]
        )
        copy.start()
        copies.append(copy)
    for copy in copies:
        copy.wait()


def subtract_interior(mid, new, table):
    height, blocks, _ = mid.shape
    vmem = pl.BlockSpec(memory_space=pltpu.VMEM)
    rows = (height - 2 * HALO) // PARTS
    return pl.pallas_call(
        interior_kernel,
        out_shape=jax.ShapeDtypeStruct(new.shape, jnp.float32),
        in_specs=[vmem] * 3,
        out_specs=pl.BlockSpec(memory_space=pl.ANY),
        scratch_shapes=[
            window_scratch(height + 2 * HALO, blocks),
            pltpu.VMEM((height - 2 * HALO, blocks * LANES), jnp.float32),
            pltpu.VMEM((2, rows * blocks, LANES), jnp.float32),
            pltpu.SemaphoreType.DMA((PARTS,)),
        ]
        + [pltpu.VMEM((UNIT, blocks + 2 * PAD, LANES), jnp.float32)] * 4,
        compiler_params=params(),
        cost_estimate=conv_cost(*new.shape),
        name="subtract_interior",
    )(mid, new, table)


def edge_kernel(low_ref, mid_ref, high_ref, new_ref, table_ref, _, out_ref, windows, result, lines, sems, *padded):
    height, blocks, _ = mid_ref.shape
    zero_edges(padded, blocks)
    sources = [
        (low_ref, 0),
        (mid_ref, 0),
        (mid_ref, UNIT),
        (mid_ref, height - 2 * UNIT),
        (mid_ref, height - UNIT),
        (high_ref, 0),
    ]
    for u, (source, first) in enumerate(sources):
        fill_windows(source, first, padded[u % len(padded)], windows, u)

    def write(k, e, line):
        row = QUAD * k + e
        lines[row * blocks : (row + 1) * blocks, :] = line

    each = HALO // QUAD
    multiply(windows, [(0, each), (3 * UNIT // QUAD, each)], table_ref, write)
    copies = []
    for side, first in enumerate((0, height - HALO)):
        for h in range(blocks):
            result[side, :, lanes_of(h)] = (
                new_ref[first : first + HALO, lanes_of(h)].astype(jnp.float32)
                - lines[pl.ds(side * HALO * blocks + h, HALO, stride=blocks), :]
            )
        copy = pltpu.make_async_copy(
            result.at[side], out_ref.at[pl.ds(first, HALO)], sems.at[side]
        )
        copy.start()
        copies.append(copy)
    for copy in copies:
        copy.wait()


def subtract_edges(low, mid, high, new, table, difference):
    _, blocks, _ = mid.shape
    vmem = pl.BlockSpec(memory_space=pltpu.VMEM)
    return pl.pallas_call(
        edge_kernel,
        out_shape=jax.ShapeDtypeStruct(difference.shape, difference.dtype),
        in_specs=[vmem] * 5 + [pl.BlockSpec(memory_space=pl.ANY)],
        out_specs=pl.BlockSpec(memory_space=pl.ANY),
        input_output_aliases={5: 0},
        scratch_shapes=[
            window_scratch(6 * UNIT, blocks),
            pltpu.VMEM((2, HALO, blocks * LANES), jnp.float32),
            pltpu.VMEM((2 * HALO * blocks, LANES), jnp.float32),
            pltpu.SemaphoreType.DMA((2,)),
        ]
        + [pltpu.VMEM((UNIT, blocks + 2 * PAD, LANES), jnp.float32)] * 3,
        compiler_params=params(),
        cost_estimate=conv_cost(2 * HALO, new.shape[1]),
        name="subtract_edges",
    )(low, mid, high, new, table, difference)


def add_visits(patch_ref, received_ref, sums):
    sums[...] = jnp.zeros_like(sums)

    def add(v, carry):
        p = patch_ref[v]
        sums[p] = sums[p] + received_ref[v].astype(jnp.float32)
        return carry

    lax.fori_loop(0, received_ref.shape[0], add, 0, unroll=4)


def sum_cover(received, patch_of):
    smem = pl.BlockSpec(memory_space=pltpu.SMEM)
    vmem = pl.BlockSpec(memory_space=pltpu.VMEM)
    return pl.pallas_call(
        add_visits,
        out_shape=jax.ShapeDtypeStruct((PATCHES,) + received.shape[1:], jnp.float32),
        in_specs=[smem, vmem],
        out_specs=vmem,
        compiler_params=params(),
        name="sum_cover",
    )(patch_of, received)


def combine_kernel(
    patch_ref, wanted_ref, received_ref, cover_ref, coadd_ref, send_ref, sums, packed, lines
):
    _, rows, blocks, _ = received_ref.shape
    add_visits(patch_ref, received_ref, sums)
    for p in range(PATCHES):
        ratio = sums[p] / jnp.maximum(cover_ref[p], 1.0)
        packed[p] = ratio.astype(jnp.bfloat16)
        lines[p] = ratio.reshape(rows * blocks, LANES)
        for h in range(blocks):
            coadd_ref[p, :, lanes_of(h)] = lines[p, pl.ds(h, rows, stride=blocks), :].astype(
                jnp.bfloat16
            )

    def place(n, carry):
        send_ref[n] = packed[wanted_ref[n]]
        return carry

    lax.fori_loop(0, send_ref.shape[0], place, 0, unroll=4)


def combine(received, cover_sums, patch_of, new_patch):
    _, rows, blocks, _ = received.shape
    smem = pl.BlockSpec(memory_space=pltpu.SMEM)
    vmem = pl.BlockSpec(memory_space=pltpu.VMEM)
    return pl.pallas_call(
        combine_kernel,
        out_shape=(
            jax.ShapeDtypeStruct((PATCHES, rows, blocks * LANES), jnp.bfloat16),
            jax.ShapeDtypeStruct((new_patch.shape[0], rows, blocks, LANES), jnp.bfloat16),
        ),
        in_specs=[smem, smem, vmem, vmem],
        out_specs=(vmem, vmem),
        scratch_shapes=[
            pltpu.VMEM((PATCHES, rows, blocks, LANES), jnp.float32),
            pltpu.VMEM((PATCHES, rows, blocks, LANES), jnp.bfloat16),
            pltpu.VMEM((PATCHES, rows * blocks, LANES), jnp.float32),
        ],
        compiler_params=params(),
        name="combine",
    )(patch_of, new_patch, received, cover_sums)


def exchange(lines):
    owners = lax.axis_size("visit")
    chunks = lines.reshape((owners, -1) + lines.shape[-2:])
    return lax.all_to_all(chunks, "visit", split_axis=0, concat_axis=0, tiled=True)


def per_device(
    visit_image,
    good_mask,
    basis_rows,
    basis_cols,
    visit_coeff,
    visit_weight,
    col_offset,
    patch_of,
    new_image,
    new_coeff,
    new_patch,
):
    low, high = neighbours(visit_image[0], "tile")
    cover = cover_rows(col_offset, visit_weight, good_mask[0])
    operands = (low, visit_image[0], high, cover, basis_rows.T, basis_cols.T, visit_coeff)
    weighted = match_visit(0, col_offset, visit_weight, operands)
    cover, weighted = lax.optimization_barrier((cover, weighted))
    received_cover = exchange(cover)
    weighted = match_visit(1, col_offset, visit_weight, operands, weighted)
    received = exchange(weighted)
    cover_sums = sum_cover(received_cover, patch_of[:, 0])
    new_coeff, cover_sums = lax.optimization_barrier((new_coeff, cover_sums))
    new_table = build_table(basis_rows, basis_cols, new_coeff)
    new_table, cover_sums = lax.optimization_barrier((new_table, cover_sums))
    coadd, wanted = combine(received, cover_sums, patch_of[:, 0], new_patch[:, 0])
    template = exchange(wanted)
    template = template.reshape((-1,) + template.shape[2:])
    low, high = neighbours(template, "tile")
    difference = subtract_interior(template, new_image[0], new_table)
    difference = subtract_edges(low, template, high, new_image[0], new_table, difference)
    return (coadd[:, None], difference[None])


def solution(mesh):
    return jax.shard_map(
        per_device,
        mesh=mesh,
        in_specs=(
            P("visit", "tile", None),
            P("visit", "tile", None),
            P(),
            P(),
            P("visit", None),
            P("visit"),
            P("visit"),
            P(),
            P("visit", "tile", None),
            P("visit", None),
            P(),
        ),
        out_specs=(P(None, "tile", "visit", None), P("visit", "tile", None)),
        check_vma=False,
    )
```

```python
import functools

import jax
import jax.numpy as jnp
from jax import lax
from jax.experimental import pallas as pl
from jax.experimental.pallas import tpu as pltpu
from jax.sharding import PartitionSpec as P

KS = 21
HALF = KS // 2
PATCHES = 8
LANES = 128
HALO = 16
QUAD = 4
SPLIT = LANES // 2
SHIFTS = QUAD + KS - 1
CHUNK = 64
PARTS = 4
UNIT = 16
PAD = 8
VMEM_LIMIT = 16 * 2**20


def params():
    return pltpu.CompilerParams(vmem_limit_bytes=VMEM_LIMIT)


def roomy():
    return pltpu.CompilerParams(vmem_limit_bytes=56 * 2**20)


def neighbours(block, axis, *after):
    count = lax.axis_size(axis)
    forward = [(i, i + 1) for i in range(count - 1)]
    backward = [(target, source) for source, target in forward]
    top, bottom = block[:HALO], block[-HALO:]
    if after:
        top, bottom, *after = lax.optimization_barrier((top, bottom, *after))
    low = lax.ppermute(bottom, axis, forward)
    high = lax.ppermute(top, axis, backward)
    return low, high, *after


def fill_table(rows_ref, cols_ref, coeff_ref, table_ref):
    wide = QUAD * SPLIT
    tap = lax.broadcasted_iota(jnp.int32, (KS, wide), 0)
    place = lax.broadcasted_iota(jnp.int32, (KS, wide), 1)
    shift = lax.broadcasted_iota(jnp.int32, (SHIFTS, KS), 0)
    row_tap = lax.broadcasted_iota(jnp.int32, (SHIFTS, KS), 1)
    lane = lax.broadcasted_iota(jnp.int32, (LANES, wide), 0)
    column = lax.broadcasted_iota(jnp.int32, (LANES, wide), 1) % SPLIT
    inside = (lane >= column) & (lane - column < KS)
    kernel = lax.dot_general(
        rows_ref[...] * coeff_ref[...],
        cols_ref[...],
        (((1,), (1,)), ((), ())),
        precision=lax.Precision.HIGHEST,
        preferred_element_type=jnp.float32,
    ).astype(jnp.bfloat16)
    profile = jnp.zeros((SHIFTS, wide), jnp.float32)
    for e in range(QUAD):
        at = (SPLIT * e - tap) % wide
        spread = jnp.dot(
            kernel, (place == at).astype(jnp.bfloat16), preferred_element_type=jnp.float32
        )
        lowered = (shift - e == row_tap).astype(jnp.bfloat16)
        profile = profile + jnp.dot(
            lowered, spread.astype(jnp.bfloat16), preferred_element_type=jnp.float32
        )
    for s in range(SHIFTS):
        line = jnp.broadcast_to(profile[s : s + 1], (LANES, wide))
        rolled = pltpu.roll(line, 0, 1, stride=1, stride_axis=0)
        table_ref[s * LANES : (s + 1) * LANES, :] = jnp.where(inside, rolled, 0.0).astype(
            jnp.bfloat16
        )


def build_table(basis_rows, basis_cols, coeff):
    return pl.pallas_call(
        fill_table,
        out_shape=jax.ShapeDtypeStruct((SHIFTS * LANES, QUAD * SPLIT), jnp.bfloat16),
        compiler_params=params(),
        cost_estimate=pl.CostEstimate(flops=10**9, bytes_accessed=2 * 10**6, transcendentals=0),
        name="table",
    )(basis_rows.T, basis_cols.T, coeff)


def split_shift(shift):
    turn = lax.rem(shift + 2 * LANES, LANES)
    return turn, (turn - shift) // LANES


def lay_out(blocks_of, shift, lines, base, pitch):
    turn, back = split_shift(shift)
    count = blocks_of[0].shape[0]
    lane = lax.broadcasted_iota(jnp.int32, (count, LANES), 1)
    before = jnp.zeros((count, LANES), blocks_of[0].dtype)
    for k in range(len(blocks_of) + 1):
        here = pltpu.roll(blocks_of[k], turn, 1) if k < len(blocks_of) else jnp.zeros_like(before)
        lines[pl.ds(base + k - back, count, stride=pitch), :] = jnp.where(
            lane >= turn, here, before
        )
        before = here


def lanes_of(h):
    return slice(h * LANES, (h + 1) * LANES)


def multiply(windows, starts, table_ref, write):
    parts = []
    for s in range(SHIFTS):
        at = s + HALO - HALF
        pieces = [
            windows[first + at // QUAD : first + at // QUAD + count, at % QUAD]
            for first, count in starts
        ]
        part = pieces[0] if len(pieces) == 1 else jnp.concatenate(pieces, axis=0)
        parts.append(part.reshape(-1, LANES))
    product = jnp.dot(
        jnp.concatenate(parts, axis=1), table_ref[...], preferred_element_type=jnp.float32
    )
    blocks = windows.shape[2] // 2
    lane = lax.broadcasted_iota(jnp.int32, (blocks, LANES), 1)
    for k in range(sum(count for _, count in starts)):
        for pair in range(QUAD // 2):
            a = product[(2 * k) * blocks : (2 * k + 1) * blocks, lanes_of(pair)]
            b = product[(2 * k + 1) * blocks : (2 * k + 2) * blocks, lanes_of(pair)]
            crossed = pltpu.roll(jnp.where(lane < SPLIT, b, a), SPLIT, 1)
            write(k, 2 * pair, jnp.where(lane < SPLIT, a, crossed))
            write(k, 2 * pair + 1, jnp.where(lane < SPLIT, crossed, b))


def lay_out_unit(source, first, shift, spot, windows, unit):
    blocks = windows.shape[2] // 2
    pitch = 4 * blocks
    pixels = [source[first : first + UNIT, lanes_of(h)].astype(jnp.float32) for h in range(blocks)]
    lay_out(pixels, shift, spot, PAD, pitch)
    lay_out(pixels, shift - SPLIT, spot, PAD + 2 * blocks, pitch)
    tiles = spot[...].reshape(UNIT, pitch, LANES)
    both = [tiles[:, PAD + 2 * blocks * k : PAD + 2 * blocks * k + blocks] for k in range(2)]
    windows[unit * (UNIT // QUAD) : (unit + 1) * (UNIT // QUAD)] = (
        jnp.concatenate(both, axis=1)
        .astype(jnp.bfloat16)
        .reshape(UNIT // QUAD, QUAD, 2 * blocks, LANES)
    )


def start_copies(pairs, sems):
    copies = [
        pltpu.make_async_copy(source, target, sems.at[i])
        for i, (source, target) in enumerate(pairs)
    ]
    for copy in copies:
        copy.start()
    return copies


def weigh(line, cover, weight):
    good = cover.astype(jnp.float32) > 0
    return (line * jnp.where(good, weight, 0.0)).astype(jnp.bfloat16)


def match_kernel(turn, *refs):
    offset_ref, weight_ref = refs[:2]
    operands = refs[2:7]
    out_ref, windows, table_ref, result, sems, *rest = refs[7 if turn == 0 else 8 :]
    held, lines = rest[:5], rest[5:]

    @pl.when(lax.axis_index("tile") % 2 == 1 - turn)
    def _():
        for copy in start_copies(zip(operands, held), sems):
            copy.wait()
        mid, cover, rows, cols, coeff = held
        fill_table(rows, cols, coeff, table_ref)
        height = mid.shape[0]
        weight = weight_ref[0]
        shift = offset_ref[0] + HALF
        each = (height - 2 * HALO) // PARTS
        done = 0
        copies = []
        for part in range(PARTS):
            first = HALO + part * each
            needed = min(-(-(first + each + HALF + 1) // UNIT), height // UNIT)
            for u in range(done, needed):
                lay_out_unit(mid, u * UNIT, shift, lines[u % len(lines)], windows, u + 1)
            done = needed

            def write(k, e, line, first=first):
                r = first + QUAD * k + e
                result[r] = weigh(line, cover[r], weight)

            multiply(windows, [(first // QUAD, each // QUAD)], table_ref, write)
            span = pl.ds(first, each)
            copy = pltpu.make_async_copy(result.at[span], out_ref.at[span], sems.at[part])
            copy.start()
            copies.append(copy)
        for copy in copies:
            copy.wait()


def match_edge_kernel(
    offset_ref, weight_ref, low, mid, high, cover, rows, cols, coeff, _, out_ref, windows, table_ref, result, sems, *lines
):
    height = mid.shape[0]
    weight = weight_ref[0]
    shift = offset_ref[0] + HALF
    fill_table(rows, cols, coeff, table_ref)
    sources = [
        (low, 0),
        (mid, 0),
        (mid, UNIT),
        (mid, height - 2 * UNIT),
        (mid, height - UNIT),
        (high, 0),
    ]
    for u, (source, first) in enumerate(sources):
        lay_out_unit(source, first, shift, lines[u % len(lines)], windows, u)
    each = HALO // QUAD

    def write(k, e, line):
        side, row = k // each, QUAD * (k % each) + e
        result[side, row] = weigh(line, cover[row + side * (height - HALO)], weight)

    multiply(windows, [(0, each), (3 * UNIT // QUAD, each)], table_ref, write)
    ends = [
        (result.at[side], out_ref.at[pl.ds(first, HALO)])
        for side, first in enumerate((0, height - HALO))
    ]
    for copy in start_copies(ends, sems):
        copy.wait()


def cover_kernel(offset_ref, weight_ref, mask_ref, out_ref, held, sems, *lines):
    height, columns = mask_ref.shape
    blocks = columns // LANES
    weight = weight_ref[0]
    spans = [pl.ds(first, CHUNK) for first in range(0, height, CHUNK)]
    copies = start_copies([(mask_ref.at[s], held.at[s]) for s in spans], sems)
    for u in range(height // UNIT):
        if u % (CHUNK // UNIT) == 0:
            copies[u // (CHUNK // UNIT)].wait()
        spot = lines[u % len(lines)]
        rows = slice(u * UNIT, (u + 1) * UNIT)
        good = [held[rows, lanes_of(h)].astype(jnp.float32) * weight for h in range(blocks)]
        lay_out(good, offset_ref[0], spot, PAD, 2 * blocks)
        tiles = spot[...].reshape(UNIT, 2 * blocks, LANES)
        out_ref[rows] = tiles[:, PAD : PAD + blocks].astype(jnp.bfloat16)


def cover_rows(offset, weight, mask):
    height, columns = mask.shape
    blocks = columns // LANES
    smem = pl.BlockSpec(memory_space=pltpu.SMEM)
    vmem = pl.BlockSpec(memory_space=pltpu.VMEM)
    return pl.pallas_call(
        cover_kernel,
        out_shape=jax.ShapeDtypeStruct((height, blocks, LANES), jnp.bfloat16),
        in_specs=[smem, smem, pl.BlockSpec(memory_space=pl.ANY)],
        out_specs=vmem,
        scratch_shapes=[
            pltpu.VMEM(mask.shape, mask.dtype),
            pltpu.SemaphoreType.DMA((height // CHUNK,)),
        ]
        + [pltpu.VMEM((UNIT * 2 * blocks, LANES), jnp.float32)] * 4,
        compiler_params=roomy(),
        cost_estimate=pl.CostEstimate(flops=10**6, bytes_accessed=6 * 10**6, transcendentals=0),
        name="cover_rows",
    )(offset, weight, mask)


def window_scratch(height, blocks):
    return pltpu.VMEM((height // QUAD, QUAD, 2 * blocks, LANES), jnp.bfloat16)


def conv_cost(height, columns):
    return pl.CostEstimate(
        flops=2 * height * columns * SHIFTS * LANES, bytes_accessed=8 * 10**6, transcendentals=0
    )


def match_visit(turn, offset, weight, operands, *before):
    height, columns = operands[0].shape
    blocks = columns // LANES
    smem = pl.BlockSpec(memory_space=pltpu.SMEM)
    anywhere = pl.BlockSpec(memory_space=pl.ANY)
    rows = (height, blocks, LANES)
    return pl.pallas_call(
        functools.partial(match_kernel, turn),
        out_shape=jax.ShapeDtypeStruct(rows, jnp.bfloat16),
        in_specs=[smem, smem] + [anywhere] * (len(operands) + len(before)),
        out_specs=anywhere,
        input_output_aliases={7: 0} if before else {},
        scratch_shapes=[
            window_scratch(height + 2 * HALO, blocks),
            pltpu.VMEM((SHIFTS * LANES, QUAD * SPLIT), jnp.bfloat16),
            pltpu.VMEM(rows, jnp.bfloat16),
            pltpu.SemaphoreType.DMA((len(operands),)),
        ]
        + [pltpu.VMEM(a.shape, a.dtype) for a in operands]
        + [pltpu.VMEM((UNIT * 4 * blocks, LANES), jnp.float32)] * 4,
        compiler_params=roomy(),
        cost_estimate=conv_cost(height, columns),
        name="match_visit",
    )(offset, weight, *operands, *before)


def match_edges(low, mid, high, cover, basis, offset, weight, weighted):
    _, columns = mid.shape
    blocks = columns // LANES
    smem = pl.BlockSpec(memory_space=pltpu.SMEM)
    vmem = pl.BlockSpec(memory_space=pltpu.VMEM)
    anywhere = pl.BlockSpec(memory_space=pl.ANY)
    return pl.pallas_call(
        match_edge_kernel,
        out_shape=jax.ShapeDtypeStruct(weighted.shape, weighted.dtype),
        in_specs=[smem, smem] + [vmem] * 7 + [anywhere],
        out_specs=anywhere,
        input_output_aliases={9: 0},
        scratch_shapes=[
            window_scratch(6 * UNIT, blocks),
            pltpu.VMEM((SHIFTS * LANES, QUAD * SPLIT), jnp.bfloat16),
            pltpu.VMEM((2, HALO, blocks, LANES), jnp.bfloat16),
            pltpu.SemaphoreType.DMA((2,)),
        ]
        + [pltpu.VMEM((UNIT * 4 * blocks, LANES), jnp.float32)] * 3,
        compiler_params=roomy(),
        cost_estimate=conv_cost(2 * HALO, columns),
        name="match_edges",
    )(offset, weight, low, mid, high, cover, *basis, weighted)


def fill_windows(source, first, padded, windows, unit):
    blocks = source.shape[1]
    turn = SPLIT + HALF
    lane = lax.broadcasted_iota(jnp.int32, (UNIT, blocks, LANES), 2)
    here = source[first : first + UNIT].astype(jnp.float32)
    padded[:, PAD : PAD + blocks] = here
    before = padded[:, PAD - 1 : PAD - 1 + blocks]
    after = padded[:, PAD + 1 : PAD + 1 + blocks]
    left = pltpu.roll(jnp.where(lane < LANES - HALF, here, before), HALF, 2)
    right = pltpu.roll(jnp.where(lane < LANES - turn, after, here), turn, 2)
    both = jnp.concatenate([left, right], axis=1).astype(jnp.bfloat16)
    windows[unit * (UNIT // QUAD) : (unit + 1) * (UNIT // QUAD)] = both.reshape(
        UNIT // QUAD, QUAD, 2 * blocks, LANES
    )


def zero_edges(padded, blocks):
    edge = jnp.zeros((UNIT, PAD, LANES), jnp.float32)
    for spot in padded:
        spot[:, :PAD] = edge
        spot[:, PAD + blocks :] = edge


def interior_kernel(mid_ref, new_ref, table_ref, out_ref, windows, result, lines, sems, *padded):
    height, blocks, _ = mid_ref.shape
    zero_edges(padded, blocks)
    rows = (height - 2 * HALO) // PARTS
    copies = []
    done = 0
    for part in range(PARTS):
        first = HALO + part * rows
        needed = -(-(first + rows + HALF + 1) // UNIT)
        for u in range(done, min(needed, height // UNIT)):
            fill_windows(mid_ref, u * UNIT, padded[u % len(padded)], windows, u + 1)
        done = needed
        spot = lines.at[part % 2]

        def write(k, e, line, spot=spot):
            row = QUAD * k + e
            spot[row * blocks : (row + 1) * blocks, :] = line

        multiply(windows, [(first // QUAD, rows // QUAD)], table_ref, write)
        for h in range(blocks):
            result[first - HALO : first - HALO + rows, lanes_of(h)] = (
                new_ref[first : first + rows, lanes_of(h)].astype(jnp.float32)
                - spot[pl.ds(h, rows, stride=blocks), :]
            )
        copy = pltpu.make_async_copy(
            result.at[pl.ds(first - HALO, rows)], out_ref.at[pl.ds(first, rows)], sems.at[part]
        )
        copy.start()
        copies.append(copy)
    for copy in copies:
        copy.wait()


def subtract_interior(mid, new, table):
    height, blocks, _ = mid.shape
    vmem = pl.BlockSpec(memory_space=pltpu.VMEM)
    rows = (height - 2 * HALO) // PARTS
    return pl.pallas_call(
        interior_kernel,
        out_shape=jax.ShapeDtypeStruct(new.shape, jnp.float32),
        in_specs=[vmem] * 3,
        out_specs=pl.BlockSpec(memory_space=pl.ANY),
        scratch_shapes=[
            window_scratch(height + 2 * HALO, blocks),
            pltpu.VMEM((height - 2 * HALO, blocks * LANES), jnp.float32),
            pltpu.VMEM((2, rows * blocks, LANES), jnp.float32),
            pltpu.SemaphoreType.DMA((PARTS,)),
        ]
        + [pltpu.VMEM((UNIT, blocks + 2 * PAD, LANES), jnp.float32)] * 4,
        compiler_params=params(),
        cost_estimate=conv_cost(*new.shape),
        name="subtract_interior",
    )(mid, new, table)


def edge_kernel(low_ref, mid_ref, high_ref, new_ref, table_ref, _, out_ref, windows, result, lines, sems, *padded):
    height, blocks, _ = mid_ref.shape
    zero_edges(padded, blocks)
    sources = [
        (low_ref, 0),
        (mid_ref, 0),
        (mid_ref, UNIT),
        (mid_ref, height - 2 * UNIT),
        (mid_ref, height - UNIT),
        (high_ref, 0),
    ]
    for u, (source, first) in enumerate(sources):
        fill_windows(source, first, padded[u % len(padded)], windows, u)

    def write(k, e, line):
        row = QUAD * k + e
        lines[row * blocks : (row + 1) * blocks, :] = line

    each = HALO // QUAD
    multiply(windows, [(0, each), (3 * UNIT // QUAD, each)], table_ref, write)
    copies = []
    for side, first in enumerate((0, height - HALO)):
        for h in range(blocks):
            result[side, :, lanes_of(h)] = (
                new_ref[first : first + HALO, lanes_of(h)].astype(jnp.float32)
                - lines[pl.ds(side * HALO * blocks + h, HALO, stride=blocks), :]
            )
        copy = pltpu.make_async_copy(
            result.at[side], out_ref.at[pl.ds(first, HALO)], sems.at[side]
        )
        copy.start()
        copies.append(copy)
    for copy in copies:
        copy.wait()


def subtract_edges(low, mid, high, new, table, difference):
    _, blocks, _ = mid.shape
    vmem = pl.BlockSpec(memory_space=pltpu.VMEM)
    return pl.pallas_call(
        edge_kernel,
        out_shape=jax.ShapeDtypeStruct(difference.shape, difference.dtype),
        in_specs=[vmem] * 5 + [pl.BlockSpec(memory_space=pl.ANY)],
        out_specs=pl.BlockSpec(memory_space=pl.ANY),
        input_output_aliases={5: 0},
        scratch_shapes=[
            window_scratch(6 * UNIT, blocks),
            pltpu.VMEM((2, HALO, blocks * LANES), jnp.float32),
            pltpu.VMEM((2 * HALO * blocks, LANES), jnp.float32),
            pltpu.SemaphoreType.DMA((2,)),
        ]
        + [pltpu.VMEM((UNIT, blocks + 2 * PAD, LANES), jnp.float32)] * 3,
        compiler_params=params(),
        cost_estimate=conv_cost(2 * HALO, new.shape[1]),
        name="subtract_edges",
    )(low, mid, high, new, table, difference)


def add_visits(patch_ref, received_ref, sums):
    sums[...] = jnp.zeros_like(sums)

    def add(v, carry):
        p = patch_ref[v]
        sums[p] = sums[p] + received_ref[v].astype(jnp.float32)
        return carry

    lax.fori_loop(0, received_ref.shape[0], add, 0, unroll=4)


def sum_cover(received, patch_of):
    smem = pl.BlockSpec(memory_space=pltpu.SMEM)
    vmem = pl.BlockSpec(memory_space=pltpu.VMEM)
    return pl.pallas_call(
        add_visits,
        out_shape=jax.ShapeDtypeStruct((PATCHES,) + received.shape[1:], jnp.float32),
        in_specs=[smem, vmem],
        out_specs=vmem,
        compiler_params=params(),
        name="sum_cover",
    )(patch_of, received)


def combine_kernel(
    patch_ref, wanted_ref, received_ref, cover_ref, coadd_ref, send_ref, sums, packed, lines
):
    _, rows, blocks, _ = received_ref.shape
    add_visits(patch_ref, received_ref, sums)
    for p in range(PATCHES):
        ratio = sums[p] / jnp.maximum(cover_ref[p], 1.0)
        packed[p] = ratio.astype(jnp.bfloat16)
        lines[p] = ratio.reshape(rows * blocks, LANES)
        for h in range(blocks):
            coadd_ref[p, :, lanes_of(h)] = lines[p, pl.ds(h, rows, stride=blocks), :].astype(
                jnp.bfloat16
            )

    def place(n, carry):
        send_ref[n] = packed[wanted_ref[n]]
        return carry

    lax.fori_loop(0, send_ref.shape[0], place, 0, unroll=4)


def combine(received, cover_sums, patch_of, new_patch):
    _, rows, blocks, _ = received.shape
    smem = pl.BlockSpec(memory_space=pltpu.SMEM)
    vmem = pl.BlockSpec(memory_space=pltpu.VMEM)
    return pl.pallas_call(
        combine_kernel,
        out_shape=(
            jax.ShapeDtypeStruct((PATCHES, rows, blocks * LANES), jnp.bfloat16),
            jax.ShapeDtypeStruct((new_patch.shape[0], rows, blocks, LANES), jnp.bfloat16),
        ),
        in_specs=[smem, smem, vmem, vmem],
        out_specs=(vmem, vmem),
        scratch_shapes=[
            pltpu.VMEM((PATCHES, rows, blocks, LANES), jnp.float32),
            pltpu.VMEM((PATCHES, rows, blocks, LANES), jnp.bfloat16),
            pltpu.VMEM((PATCHES, rows * blocks, LANES), jnp.float32),
        ],
        compiler_params=params(),
        name="combine",
    )(patch_of, new_patch, received, cover_sums)


def exchange(lines):
    owners = lax.axis_size("visit")
    chunks = lines.reshape((owners, -1) + lines.shape[-2:])
    return lax.all_to_all(chunks, "visit", split_axis=0, concat_axis=0, tiled=True)


def per_device(
    visit_image,
    good_mask,
    basis_rows,
    basis_cols,
    visit_coeff,
    visit_weight,
    col_offset,
    patch_of,
    new_image,
    new_coeff,
    new_patch,
):
    low, high = neighbours(visit_image[0], "tile")
    cover = cover_rows(col_offset, visit_weight, good_mask[0])
    basis = (basis_rows.T, basis_cols.T, visit_coeff)
    operands = (visit_image[0], cover, *basis)
    weighted = match_visit(0, col_offset, visit_weight, operands)
    cover, weighted = lax.optimization_barrier((cover, weighted))
    received_cover = exchange(cover)
    weighted = match_visit(1, col_offset, visit_weight, operands, weighted)
    weighted = match_edges(
        low, visit_image[0], high, cover, basis, col_offset, visit_weight, weighted
    )
    received = exchange(weighted)
    cover_sums = sum_cover(received_cover, patch_of[:, 0])
    new_coeff, cover_sums = lax.optimization_barrier((new_coeff, cover_sums))
    new_table = build_table(basis_rows, basis_cols, new_coeff)
    new_table, cover_sums = lax.optimization_barrier((new_table, cover_sums))
    coadd, wanted = combine(received, cover_sums, patch_of[:, 0], new_patch[:, 0])
    template = exchange(wanted)
    template = template.reshape((-1,) + template.shape[2:])
    low, high = neighbours(template, "tile")
    difference = subtract_interior(template, new_image[0], new_table)
    difference = subtract_edges(low, template, high, new_image[0], new_table, difference)
    return (coadd[:, None], difference[None])


def solution(mesh):
    return jax.shard_map(
        per_device,
        mesh=mesh,
        in_specs=(
            P("visit", "tile", None),
            P("visit", "tile", None),
            P(),
            P(),
            P("visit", None),
            P("visit"),
            P("visit"),
            P(),
            P("visit", "tile", None),
            P("visit", None),
            P(),
        ),
        out_specs=(P(None, "tile", "visit", None), P("visit", "tile", None)),
        check_vma=False,
    )
```
